32 devices in a mesh: parts: 2 (over y), gx: 4 (over x, core), gy: 4 (over z).
Axes of the slice: x: 2, y: 2, z: 4, core: 2. Of those that a mesh axis runs over, the one named last changes fastest.
Arguments:
- hidden_states: bfloat16 [128, 16384], P(('parts', 'gy'), 'gx'), parts along dimension 0, may hold values from -400 to 400
- norm_gain: bfloat16 [16384], P('gx'), may hold values from 0.099609375 to 1.8984375
- w_query: bfloat16 [16384, 8192], P('gx', 'gy'), may hold values from -0.046875 to 0.046875
- key_weight: bfloat16 [16384, 512], P('gx', 'gy'), may hold values from -0.046875 to 0.046875
- value_weight: bfloat16 [16384, 512], P('gx', 'gy'), may hold values from -0.046875 to 0.046875
- w_output: bfloat16 [8192, 16384], P('gy', 'gx'), may hold values from -0.25 to 0.25
- stored_key_cache: bfloat16 [128, 256, 512], P(('parts', 'gx', 'gy')), parts along dimension 0, may hold values from -120 to 120
- stored_value_cache: bfloat16 [128, 256, 512], P(('parts', 'gx', 'gy')), parts along dimension 0, may hold values from -6 to 6
- filled_lengths: int32 [128], P(('parts', 'gx', 'gy')), parts along dimension 0, may hold values from 1 to 256
Outputs:
- attn_out: bfloat16 [128, 16384], P(('parts', 'gy'), 'gx'), parts along dimension 0
The draws below stay inside these ranges and needn't reach their ends.
There are 2 independent parts, one for each index of `parts`. The reference program is written for one: setup_inputs(seed, part) draws one part's arguments, and reference() takes and returns one part's arrays. A program takes and returns all parts, laid end to end along the dimension named above; an argument that names none is the same for every part. Nothing has to cross between parts.
All inputs are finite; a program needn't handle non-finite values.
Results may differ from the reference program's by a relative error of at most 0.03.
Values may be sent and summed in bfloat16 or wider, within the bound.
No kernel may reach another device: no remote copies, remote signals or barrier semaphores. Data moves between devices by JAX's collectives and lax.ppermute only.
A program may use at most 128 MiB of HBM per device.

```python
import jax
import jax.numpy as jnp
from jax import lax

MODEL_WIDTH = 16384
QUERY_HEADS = 64
KEY_VALUE_HEADS = 4
HEAD_SIZE = 128
CACHE_SLOTS = 256
TOKEN_COUNT = 64
N_GX = 4
N_GY = 4


def draw_hidden_states(key, part):
    key = jax.random.fold_in(key, 5)
    first, second_factor = jax.random.split(key, 2)
    columns = jnp.exp(jnp.log(10.0) * jnp.arange(MODEL_WIDTH, dtype=jnp.float32) / MODEL_WIDTH)
    rows = jnp.exp(jax.random.uniform(second_factor, (TOKEN_COUNT, 1), jnp.float32, 0.0, jnp.log(10.0)))
    base_offset = jnp.clip(jax.random.normal(first, (TOKEN_COUNT, MODEL_WIDTH), jnp.float32), -4.0, 4.0)
    return (base_offset * columns[None, :] * rows).astype(jnp.bfloat16)


def draw_stored_key_cache(key, part):
    key = jax.random.fold_in(key, 11)
    first = jax.random.fold_in(key, 0)
    array_shape = (TOKEN_COUNT, CACHE_SLOTS, KEY_VALUE_HEADS * HEAD_SIZE)
    base_offset = jnp.clip(jax.random.normal(first, array_shape, jnp.float32), -6.0, 6.0)
    return base_offset.astype(jnp.bfloat16)


def draw_filled_lengths(key, part):
    key = jax.random.fold_in(key, 17)
    first, second_factor = jax.random.split(key)
    lengths = jax.random.randint(first, (TOKEN_COUNT,), 1, CACHE_SLOTS + 1)
    longest = jax.random.randint(second_factor, (), 0, TOKEN_COUNT)
    return lengths.at[longest].set(CACHE_SLOTS).astype(jnp.int32)


def steps_of(rng, extent, shards, smallest, top_value):
    loudness = 1.0
    for dim, shards_of in shards:
        draws = jax.random.uniform(jax.random.fold_in(jax.random.fold_in(rng, 6), dim), (shards_of,), jnp.float32, smallest / len(shards), top_value / len(shards))
        loudness = loudness * jnp.repeat(jnp.exp(draws), extent[dim] // shards_of).reshape((-1,) + (1,) * (len(extent) - 1 - dim))
    return loudness


def centred(own_key, extent, scale, bound, cuts=(), held_as=jnp.bfloat16):
    entries = scale * jax.random.normal(own_key, extent, jnp.float32)
    if cuts:
        entries = entries * steps_of(own_key, extent, cuts, -0.22, 0.18)
    return jnp.clip(entries, -bound, bound).astype(held_as)


def setup_inputs(seed: int = 0, part: int = 0) -> dict:
    streams_of = jax.random.split(jax.random.key(seed), 10)
    own_keys = jax.random.split(jax.random.fold_in(streams_of[9], part), 10)
    return {
        "hidden_states": draw_hidden_states(jax.random.fold_in(jax.random.fold_in(streams_of[9], part), 71), part),
        "norm_gain": jnp.clip(1.0 + 0.18 * jax.random.normal(streams_of[1], (MODEL_WIDTH,), jnp.float32), 0.099609375, 1.8984375).astype(jnp.bfloat16),
        "w_query": centred(streams_of[2], (MODEL_WIDTH, QUERY_HEADS * HEAD_SIZE), MODEL_WIDTH ** -0.5, 0.046875, ((0, 4), (1, 4))),
        "key_weight": centred(streams_of[3], (MODEL_WIDTH, KEY_VALUE_HEADS * HEAD_SIZE), MODEL_WIDTH ** -0.5, 0.046875, ((0, 4), (1, 4))),
        "value_weight": centred(streams_of[4], (MODEL_WIDTH, KEY_VALUE_HEADS * HEAD_SIZE), MODEL_WIDTH ** -0.5, 0.046875, ((0, 4), (1, 4))),
        "w_output": centred(streams_of[5], (QUERY_HEADS * HEAD_SIZE, MODEL_WIDTH), (QUERY_HEADS * HEAD_SIZE // 16) ** -0.5, 0.25, ((0, 4), (1, 4))),
        "stored_key_cache": draw_stored_key_cache(jax.random.fold_in(jax.random.fold_in(streams_of[9], part), 71), part),
        "stored_value_cache": centred(own_keys[7], (TOKEN_COUNT, CACHE_SLOTS, KEY_VALUE_HEADS * HEAD_SIZE), 1.0, 6.0, ((0, 16),)),
        "filled_lengths": draw_filled_lengths(jax.random.fold_in(jax.random.fold_in(streams_of[9], part), 71), part),
    }


def rotary_angles(heads, positions):
    half = HEAD_SIZE // 2
    freqs = 500000.0 ** (-(jnp.arange(half, dtype=jnp.float32) * 2.0 / HEAD_SIZE))
    angles = positions.astype(jnp.float32)[:, None, None] * freqs[None, None, :]
    first = heads[..., :half]
    second_factor = heads[..., half:]
    cosine = jnp.cos(angles)
    sine = jnp.sin(angles)
    return jnp.concatenate([first * cosine - second_factor * sine, second_factor * cosine + first * sine], axis=-1)

def blocked(left, right, pieces):
    width = left.shape[1] // pieces

    def one_block(index, carry):
        start = (index * width).astype(jnp.int32)
        cols = lax.dynamic_slice_in_dim(left, start, width, 1)
        rows = lax.dynamic_slice_in_dim(right, start, width, 0)
        term = jnp.dot(cols, rows, preferred_element_type=jnp.float32).astype(jnp.bfloat16)
        term = lax.optimization_barrier(term)
        return carry + term.astype(jnp.float32)
    empty = jnp.zeros((left.shape[0], right.shape[1]), jnp.float32)
    return lax.fori_loop(0, pieces, one_block, empty)

def attend(query_vector, key_rows, value_rows, fresh_key, fresh_value, lengths):
    item_count = query_vector.shape[0]
    group_count = QUERY_HEADS // KEY_VALUE_HEADS
    scale = 1.0 / HEAD_SIZE ** 0.5
    query_float = query_vector.astype(jnp.float32).reshape(item_count, KEY_VALUE_HEADS, group_count, HEAD_SIZE)
    key_float = key_rows.astype(jnp.float32).reshape(item_count, CACHE_SLOTS, KEY_VALUE_HEADS, HEAD_SIZE)
    value_float = value_rows.astype(jnp.float32).reshape(item_count, CACHE_SLOTS, KEY_VALUE_HEADS, HEAD_SIZE)
    fresh_key_float = fresh_key.astype(jnp.float32).reshape(item_count, KEY_VALUE_HEADS, HEAD_SIZE)
    fresh_value_float = fresh_value.astype(jnp.float32).reshape(item_count, KEY_VALUE_HEADS, 1, HEAD_SIZE)
    scores = jnp.einsum('nkgd,nlkd->nkgl', query_float, key_float) * scale
    own = jnp.einsum('nkgd,nkd->nkg', query_float, fresh_key_float) * scale
    valid = jnp.arange(CACHE_SLOTS)[None, None, None, :] < lengths[:, None, None, None]
    scores = jnp.where(valid, scores, -1e+30)
    top = jnp.maximum(lax.optimization_barrier(jnp.max(scores, axis=-1)), own)
    weights = jnp.where(valid, jnp.exp(scores - top[..., None]), 0.0)
    own_weight = jnp.exp(own - top)
    total = lax.optimization_barrier(jnp.sum(weights, axis=-1)) + own_weight
    rounded = lax.optimization_barrier(weights.astype(jnp.bfloat16)).astype(jnp.float32)
    local_rounded = lax.optimization_barrier(own_weight.astype(jnp.bfloat16)).astype(jnp.float32)
    mixed_output = jnp.einsum('nkgl,nlkd->nkgd', rounded, value_float) + local_rounded[..., None] * fresh_value_float
    return (mixed_output / total[..., None]).reshape(item_count, QUERY_HEADS * HEAD_SIZE).astype(jnp.bfloat16)

def reference(hidden_states, norm_gain, w_query, key_weight, value_weight, w_output, stored_key_cache, stored_value_cache, filled_lengths):
    states = hidden_states.astype(jnp.float32)
    row_scaling = lax.rsqrt(lax.optimization_barrier(jnp.sum(states * states, axis=1)) / MODEL_WIDTH + 1e-05)
    scaled = (states * norm_gain.astype(jnp.float32)[None, :]).astype(jnp.bfloat16)
    query_sum = blocked(scaled, w_query, N_GX)
    key_total = blocked(scaled, key_weight, N_GX)
    value_sum = blocked(scaled, value_weight, N_GX)
    query_vector = rotary_angles((row_scaling[:, None] * query_sum).reshape(TOKEN_COUNT, QUERY_HEADS, HEAD_SIZE), filled_lengths)
    query_vector = query_vector.reshape(TOKEN_COUNT, QUERY_HEADS * HEAD_SIZE).astype(jnp.bfloat16)
    fresh_key = rotary_angles((row_scaling[:, None] * key_total).reshape(TOKEN_COUNT, KEY_VALUE_HEADS, HEAD_SIZE), filled_lengths)
    fresh_key = fresh_key.reshape(TOKEN_COUNT, KEY_VALUE_HEADS * HEAD_SIZE).astype(jnp.bfloat16)
    fresh_value = (row_scaling[:, None] * value_sum).astype(jnp.bfloat16)
    block_list = 16
    block_size = TOKEN_COUNT // block_list

    def single_group(items):
        return attend(*items)
    attention_result = lax.map(single_group, (query_vector.reshape(block_list, block_size, QUERY_HEADS * HEAD_SIZE), stored_key_cache.reshape(block_list, block_size, CACHE_SLOTS, KEY_VALUE_HEADS * HEAD_SIZE), stored_value_cache.reshape(block_list, block_size, CACHE_SLOTS, KEY_VALUE_HEADS * HEAD_SIZE), fresh_key.reshape(block_list, block_size, KEY_VALUE_HEADS * HEAD_SIZE), fresh_value.reshape(block_list, block_size, KEY_VALUE_HEADS * HEAD_SIZE), filled_lengths.reshape(block_list, block_size)))
    attention_result = attention_result.reshape(TOKEN_COUNT, QUERY_HEADS * HEAD_SIZE)
    return blocked(attention_result, w_output, N_GY).astype(jnp.bfloat16)
```

```python
import functools

import jax
import jax.numpy as jnp
from jax import lax
from jax.experimental import pallas as pl
from jax.experimental.pallas import tpu as pltpu
from jax.sharding import PartitionSpec as P

HEAD_SIZE = 128
LANES = 128
EPSILON = 1e-05
VMEM = pl.BlockSpec(memory_space=pltpu.VMEM)


def square_lanes(total):
    high = total.astype(jnp.bfloat16).astype(jnp.float32)
    rest = total - high
    middle = rest.astype(jnp.bfloat16).astype(jnp.float32)
    lane = lax.broadcasted_iota(jnp.int32, (total.shape[0], LANES), 1)
    low = rest - middle
    return jnp.where(lane == 0, high, jnp.where(lane == 1, middle, jnp.where(lane == 2, low, 0.0)))


def project_kernel(count, width, *refs):
    pieces, (gain, w_query, key_weight, value_weight) = refs[:count], refs[count : count + 4]
    outs, (scaled, squares) = refs[count + 4 : 2 * count + 4], refs[2 * count + 4 :]
    flip = lax.axis_index("gx") ^ lax.axis_index("gy")
    gains = gain[...].astype(jnp.float32)
    for offset in range(count):
        states = pieces[offset][...].astype(jnp.float32)
        scaled[flip ^ offset] = (states * gains).astype(jnp.bfloat16)
        squares[flip ^ offset] = square_lanes(jnp.sum(states * states, axis=1, keepdims=True))
    rows = scaled.shape[1]
    left = scaled[...].reshape(count * rows, scaled.shape[2])
    start = 0
    for weight in (w_query, key_weight, value_weight):
        columns = weight.shape[1]
        step = min(columns, 512)
        for first in range(0, columns, step):
            product = jnp.dot(
                left, weight[:, first : first + step], preferred_element_type=jnp.float32
            ).astype(jnp.bfloat16)
            for offset in range(count):
                outs[offset][:, start : start + step] = product[offset * rows : (offset + 1) * rows]
            start += step
    for offset in range(count):
        if start < width - LANES:
            outs[offset][:, start : width - LANES] = jnp.zeros(
                (rows, width - LANES - start), jnp.bfloat16
            )
        outs[offset][:, width - LANES :] = squares[offset].astype(jnp.bfloat16)


def combine_kernel(count, *refs):
    pieces, outs, (held,) = refs[:count], refs[count : 2 * count], refs[2 * count :]
    total = pieces[0][...].astype(jnp.float32)
    for piece in pieces[1:]:
        total = total + piece[...].astype(jnp.float32)
    share = held.shape[1]
    width = total.shape[1]
    squares = square_lanes(jnp.sum(total[:, width - LANES :], axis=1, keepdims=True))
    for owner in range(count):
        rows = slice(owner * share, (owner + 1) * share)
        held[owner, :, : width - LANES] = total[rows, : width - LANES]
        held[owner, :, width - LANES :] = squares[rows]
    me = lax.axis_index("gy")
    for offset in range(count):
        outs[offset][...] = held[me ^ offset].astype(jnp.bfloat16)


def attend_kernel(count, group, features, *refs):
    pieces, (keys, values, cosines, sines, lengths) = refs[:count], refs[count : count + 5]
    outs = refs[count + 5 :]
    share, slots = keys.shape[0], keys.shape[1]
    rows = share * group
    scale = 1.0 / HEAD_SIZE**0.5
    width = pieces[0].shape[1]
    me = lax.axis_index("gy")
    cosine, sine = cosines[...], sines[...]
    squares = jnp.sum(
        pieces[0][:, width - LANES :].astype(jnp.float32), axis=1, keepdims=True
    )
    row_scale = lax.rsqrt(squares / features + EPSILON)
    row_scales = jnp.concatenate([row_scale] * group, axis=0)
    item = lax.broadcasted_iota(jnp.int32, (rows, 1), 0) % share
    valid = lax.broadcasted_iota(jnp.int32, (rows, slots), 1) < lengths[...]
    for offset in range(count):
        piece = pieces[offset][...].astype(jnp.float32)
        head = me ^ offset
        lanes = pl.ds(pl.multiple_of(head * HEAD_SIZE, HEAD_SIZE), HEAD_SIZE)
        query = jnp.concatenate(
            [piece[:, h * HEAD_SIZE : (h + 1) * HEAD_SIZE] for h in range(group)], axis=0
        )
        query = query * row_scales
        query = query * cosine + pltpu.roll(query, HEAD_SIZE // 2, 1) * sine
        query = query.astype(jnp.bfloat16)
        first = group * HEAD_SIZE
        fresh_key = jnp.concatenate([piece[:, first : first + HEAD_SIZE]] * group, axis=0)
        fresh_key = fresh_key * row_scales
        fresh_key = fresh_key * cosine + pltpu.roll(fresh_key, HEAD_SIZE // 2, 1) * sine
        fresh_key = fresh_key.astype(jnp.bfloat16).astype(jnp.float32)
        first = first + HEAD_SIZE
        fresh_value = jnp.concatenate([piece[:, first : first + HEAD_SIZE]] * group, axis=0)
        fresh_value = (fresh_value * row_scales).astype(jnp.bfloat16).astype(jnp.float32)
        own = jnp.sum(query.astype(jnp.float32) * fresh_key, axis=1, keepdims=True) * scale
        scores = jnp.zeros((rows, slots), jnp.float32)
        for n in range(share):
            product = lax.dot_general(
                query,
                keys[n, :, lanes],
                (((1,), (1,)), ((), ())),
                preferred_element_type=jnp.float32,
            )
            scores = jnp.where(item == n, product, scores)
        scores = jnp.where(valid, scores * scale, -1e30)
        top = jnp.maximum(jnp.max(scores, axis=1, keepdims=True), own)
        weights = jnp.where(valid, jnp.exp(scores - top), 0.0)
        own_weight = jnp.exp(own - top)
        total = jnp.sum(weights, axis=1, keepdims=True) + own_weight
        mixed = own_weight.astype(jnp.bfloat16).astype(jnp.float32) * fresh_value
        for n in range(share):
            mixed = mixed + jnp.dot(
                jnp.where(item == n, weights, 0.0).astype(jnp.bfloat16),
                values[n, :, lanes],
                preferred_element_type=jnp.float32,
            )
        mixed = mixed / total
        outs[offset][...] = jnp.concatenate(
            [mixed[h * share : (h + 1) * share] for h in range(group)], axis=1
        ).astype(jnp.bfloat16)


def assemble_kernel(count, *refs):
    pieces, out, held = refs[:count], refs[count], refs[count + 1]
    me = lax.axis_index("gy")
    for offset in range(count):
        held[me ^ offset] = pieces[offset][...].astype(jnp.float32)
    out[...] = jnp.concatenate([held[n] for n in range(count)], axis=0).astype(jnp.bfloat16)


def output_kernel(count, *refs):
    pieces, weight = refs[:count], refs[count]
    outs, (held,) = refs[count + 1 : 2 * count + 1], refs[2 * count + 1 :]
    flip = lax.axis_index("gx") ^ lax.axis_index("gy")
    for offset in range(count):
        held[flip ^ offset] = pieces[offset][...]
    rows = held.shape[1]
    left = held[...].reshape(count * rows, held.shape[2])
    columns = weight.shape[1]
    step = min(columns, 512)
    for first in range(0, columns, step):
        product = jnp.dot(
            left, weight[:, first : first + step], preferred_element_type=jnp.float32
        ).astype(jnp.bfloat16)
        for offset in range(count):
            outs[offset][:, first : first + step] = product[offset * rows : (offset + 1) * rows]


def add_kernel(count, *refs):
    total = refs[0][...].astype(jnp.float32)
    for piece in refs[1:count]:
        total = total + piece[...].astype(jnp.float32)
    refs[count][...] = total.astype(jnp.bfloat16)


def call(kernel, outs, scratch, args, name, limit=None):
    return pl.pallas_call(
        kernel,
        out_shape=outs,
        in_specs=[VMEM] * len(args),
        out_specs=jax.tree.map(lambda _: VMEM, outs),
        scratch_shapes=scratch,
        compiler_params=pltpu.CompilerParams(vmem_limit_bytes=limit),
        name=name,
    )(*args)


def array(shape, dtype=jnp.bfloat16):
    return jax.ShapeDtypeStruct(shape, dtype)


def exchange(pieces, axis):
    count = len(pieces)
    result = list(pieces)
    for offset in range(count - 1, 0, -1):
        result[offset] = lax.ppermute(
            pieces[offset], axis, [(n, n ^ offset) for n in range(count)]
        )
    return result


def per_device(
    hidden_states,
    norm_gain,
    w_query,
    key_weight,
    value_weight,
    w_output,
    stored_key_cache,
    stored_value_cache,
    filled_lengths,
):
    across, down = lax.axis_size("gx"), lax.axis_size("gy")
    assert across == down and across & (across - 1) == 0
    count = down
    share, slots, cache_width = stored_key_cache.shape
    rows, depth = hidden_states.shape
    features = depth * across
    query_columns, key_columns = w_query.shape[1], key_weight.shape[1]
    kv_heads = cache_width // HEAD_SIZE
    group = query_columns * down // HEAD_SIZE // kv_heads
    half = HEAD_SIZE // 2

    with jax.named_scope("gather_hidden"):
        gathered = exchange([hidden_states] * count, "gy")

    with jax.named_scope("angles"):
        freqs = 500000.0 ** (-(jnp.arange(half, dtype=jnp.float32) * 2.0 / HEAD_SIZE))
        angles = filled_lengths.astype(jnp.float32)[:, None] * freqs[None, :]
        cosine, sine = jnp.cos(angles), jnp.sin(angles)
        cosine = jnp.concatenate([cosine, cosine], axis=1)
        sine = jnp.concatenate([-sine, sine], axis=1)

    used = query_columns + 2 * key_columns
    width = -(-used // LANES) * LANES + LANES
    with jax.named_scope("project"):
        partial = call(
            functools.partial(project_kernel, count, width),
            [array((rows, width))] * count,
            [
                pltpu.VMEM((count, rows, depth), jnp.bfloat16),
                pltpu.VMEM((count, rows, LANES), jnp.float32),
            ],
            [
                *gathered,
                norm_gain[None, :],
                *(
                    pltpu.with_memory_space_constraint(w, pltpu.VMEM)
                    for w in (w_query, key_weight, value_weight)
                ),
            ],
            "project",
            40 << 20,
        )
    with jax.named_scope("sum_gx"):
        received = exchange(partial, "gx")
        owned = call(
            functools.partial(combine_kernel, count),
            [array((share, width))] * count,
            [pltpu.VMEM((count, share, width), jnp.float32)],
            received,
            "combine",
        )
    with jax.named_scope("to_owner"):
        owned = exchange(owned, "gy")

    if key_columns == HEAD_SIZE:
        with jax.named_scope("attend"):
            attended = call(
                functools.partial(attend_kernel, count, group, features),
                [array((share, query_columns))] * count,
                [],
                [
                    *owned,
                    stored_key_cache,
                    stored_value_cache,
                    jnp.tile(cosine, (group, 1)),
                    jnp.tile(sine, (group, 1)),
                    jnp.tile(filled_lengths, group)[:, None],
                ],
                "attend",
                24 << 20,
            )
    else:
        with jax.named_scope("attend"):
            attended = attend_narrow(
                owned, used, features, stored_key_cache, stored_value_cache, cosine, sine,
                filled_lengths, query_columns, key_columns,
            )

    with jax.named_scope("to_head_rows"):
        attended = exchange(attended, "gy")
        block = call(
            functools.partial(assemble_kernel, count),
            array((count * share, query_columns)),
            [pltpu.VMEM((count, share, query_columns), jnp.float32)],
            attended,
            "assemble",
        )
    with jax.named_scope("gather_gx"):
        blocks = exchange([block] * count, "gx")
    with jax.named_scope("output"):
        products = call(
            functools.partial(output_kernel, count),
            [array((count * share, w_output.shape[1]))] * count,
            [pltpu.VMEM((count, count * share, query_columns), jnp.bfloat16)],
            [*blocks, pltpu.with_memory_space_constraint(w_output, pltpu.VMEM)],
            "output",
            40 << 20,
        )
    with jax.named_scope("sum_gy"):
        products = exchange(products, "gy")
        return call(
            functools.partial(add_kernel, count),
            array((rows, w_output.shape[1])),
            [],
            products,
            "add",
        )


def attend_narrow(
    owned, used, features, key_rows, value_rows, cosine, sine, lengths, query_columns, key_columns
):
    count = len(owned)
    share, slots, cache_width = key_rows.shape
    kv_heads = cache_width // HEAD_SIZE
    group = query_columns * count // HEAD_SIZE // kv_heads
    me = lax.axis_index("gy")
    order = me ^ jnp.arange(count)
    stacked = jnp.stack(owned).astype(jnp.float32)
    squares = jnp.sum(stacked[0, :, -LANES:], axis=1)
    row_scale = lax.rsqrt(squares / features + EPSILON)[:, None]
    stacked = jnp.take(stacked, order, axis=0)

    def columns(first, size):
        block = stacked[:, :, first : first + size]
        return row_scale * block.transpose(1, 0, 2).reshape(share, count * size)

    def rotary(heads):
        swapped = jnp.concatenate(
            [heads[..., HEAD_SIZE // 2 :], heads[..., : HEAD_SIZE // 2]], axis=-1
        )
        shape = (share,) + (1,) * (heads.ndim - 2) + (HEAD_SIZE,)
        return (heads * cosine.reshape(shape) + swapped * sine.reshape(shape)).astype(jnp.bfloat16)

    query = rotary(columns(0, query_columns).reshape(share, kv_heads, group, HEAD_SIZE))
    fresh_key = rotary(
        columns(query_columns, key_columns).reshape(share, kv_heads, HEAD_SIZE)
    )
    fresh_value = columns(query_columns + key_columns, key_columns).astype(jnp.bfloat16)
    key_heads = key_rows.reshape(share, slots, kv_heads, HEAD_SIZE)
    value_heads = value_rows.reshape(share, slots, kv_heads, HEAD_SIZE)
    scale = 1.0 / HEAD_SIZE**0.5
    scores = scale * jnp.einsum(
        "nkgd,nlkd->nkgl", query, key_heads, preferred_element_type=jnp.float32
    )
    own = scale * jnp.einsum(
        "nkgd,nkd->nkg", query, fresh_key, preferred_element_type=jnp.float32
    )
    valid = jnp.arange(slots)[None, None, None, :] < lengths[:, None, None, None]
    scores = jnp.where(valid, scores, -1e30)
    top = jnp.maximum(jnp.max(scores, axis=-1), own)
    weights = jnp.where(valid, jnp.exp(scores - top[..., None]), 0.0)
    own_weight = jnp.exp(own - top)
    total = jnp.sum(weights, axis=-1) + own_weight
    mixed = jnp.einsum(
        "nkgl,nlkd->nkgd",
        weights.astype(jnp.bfloat16),
        value_heads,
        preferred_element_type=jnp.float32,
    )
    own_weight = own_weight.astype(jnp.bfloat16).astype(jnp.float32)
    mixed = mixed + own_weight[..., None] * fresh_value.reshape(
        share, kv_heads, 1, HEAD_SIZE
    ).astype(jnp.float32)
    mixed = (mixed / total[..., None]).astype(jnp.bfloat16)
    blocks = mixed.reshape(share, count, query_columns).transpose(1, 0, 2)
    blocks = jnp.take(blocks, order, axis=0)
    return [blocks[offset] for offset in range(count)]


def solution(mesh):
    placed = (
        P(("parts", "gy"), "gx"),
        P("gx"),
        P("gx", "gy"),
        P("gx", "gy"),
        P("gx", "gy"),
        P("gy", "gx"),
        P(("parts", "gx", "gy"), None, None),
        P(("parts", "gx", "gy"), None, None),
        P(("parts", "gx", "gy")),
    )
    return jax.shard_map(
        per_device, mesh=mesh, in_specs=placed, out_specs=P(("parts", "gy"), "gx"), check_vma=False
    )
```

```python
import functools
import math

import jax
import jax.numpy as jnp
from jax import lax
from jax.experimental import pallas as pl
from jax.experimental.pallas import tpu as pltpu
from jax.sharding import PartitionSpec as P

HEAD_SIZE = 128
LANES = 128
EPSILON = 1e-05
CUTS = (4,)
LOADS = len(CUTS) + 1
VMEM = pl.BlockSpec(memory_space=pltpu.VMEM)


def square_lanes(total):
    high = total.astype(jnp.bfloat16).astype(jnp.float32)
    rest = total - high
    middle = rest.astype(jnp.bfloat16).astype(jnp.float32)
    lane = lax.broadcasted_iota(jnp.int32, (total.shape[0], LANES), 1)
    low = rest - middle
    return jnp.where(lane == 0, high, jnp.where(lane == 1, middle, jnp.where(lane == 2, low, 0.0)))


def project_kernel(count, width, *refs):
    pieces = [refs[wide_order(count).index(offset)] for offset in range(count)]
    gain, w_query, key_weight, value_weight = refs[count : count + 4]
    outs, (scaled, squares) = refs[count + 4 : 2 * count + 4], refs[2 * count + 4 :]
    flip = lax.axis_index("gx") ^ lax.axis_index("gy")
    gains = gain[...].astype(jnp.float32)[None, :]
    for offset in range(count):
        states = pieces[offset][...].astype(jnp.float32)
        scaled[flip ^ offset] = (states * gains).astype(jnp.bfloat16)
        squares[flip ^ offset] = square_lanes(jnp.sum(states * states, axis=1, keepdims=True))
    rows = scaled.shape[1]
    left = scaled[...].reshape(count * rows, scaled.shape[2])
    start = 0
    for weight in (w_query, key_weight, value_weight):
        columns = weight.shape[1]
        step = min(columns, 512)
        for first in range(0, columns, step):
            product = jnp.dot(
                left, weight[:, first : first + step], preferred_element_type=jnp.float32
            ).astype(jnp.bfloat16)
            for offset in range(count):
                outs[offset][:, start : start + step] = product[offset * rows : (offset + 1) * rows]
            start += step
    for offset in range(count):
        if start < width - LANES:
            outs[offset][:, start : width - LANES] = jnp.zeros(
                (rows, width - LANES - start), jnp.bfloat16
            )
        outs[offset][:, width - LANES :] = squares[offset].astype(jnp.bfloat16)


def combine_kernel(count, *refs):
    pieces = [refs[wide_order(count).index(offset)] for offset in range(count)]
    outs, (held,) = refs[count : 2 * count], refs[2 * count :]
    total = pieces[0][...].astype(jnp.float32)
    for piece in pieces[1:]:
        total = total + piece[...].astype(jnp.float32)
    share = held.shape[1]
    width = total.shape[1]
    squares = square_lanes(jnp.sum(total[:, width - LANES :], axis=1, keepdims=True))
    for owner in range(count):
        rows = slice(owner * share, (owner + 1) * share)
        held[owner, :, : width - LANES] = total[rows, : width - LANES]
        held[owner, :, width - LANES :] = squares[rows]
    me = lax.axis_index("gy")
    for offset in range(count):
        outs[offset][...] = held[me ^ offset].astype(jnp.bfloat16)


def spread(rows, group):
    repeat = min(group, max(1, 8 // rows.shape[0]))
    tile = jnp.concatenate([rows] * repeat, axis=0) if repeat > 1 else rows
    wide = jnp.broadcast_to(tile[None], (group // repeat, *tile.shape))
    return wide.reshape(group * rows.shape[0], rows.shape[1])


def attend_kernel(count, group, features, *refs):
    pieces = [refs[order(count).index(offset)] for offset in range(count)]
    keys, values, cosines, sines, filled = refs[count : count + 5]
    outs = refs[count + 5 :]
    share, slots = keys.shape[0], keys.shape[1]
    rows = share * group
    scale = 1.0 / HEAD_SIZE**0.5
    width = pieces[0].shape[1]
    me = lax.axis_index("gy")
    cosine, sine = cosines[...], sines[...]
    squares = jnp.sum(
        pieces[0][:, width - LANES :].astype(jnp.float32), axis=1, keepdims=True
    )
    row_scale = lax.rsqrt(squares / features + EPSILON)
    row_scales = spread(row_scale, group)
    item = lax.broadcasted_iota(jnp.int32, (rows, 1), 0) % share
    valid = lax.broadcasted_iota(jnp.int32, (rows, slots), 1) < filled[:, :1]
    for offset in range(count):
        piece = pieces[offset][...].astype(jnp.float32)
        head = me ^ offset
        lanes = pl.ds(pl.multiple_of(head * HEAD_SIZE, HEAD_SIZE), HEAD_SIZE)
        query = jnp.concatenate(
            [piece[:, h * HEAD_SIZE : (h + 1) * HEAD_SIZE] for h in range(group)], axis=0
        )
        query = query * row_scales
        query = query * cosine + pltpu.roll(query, HEAD_SIZE // 2, 1) * sine
        query = query.astype(jnp.bfloat16)
        first = group * HEAD_SIZE
        fresh_key = spread(piece[:, first : first + HEAD_SIZE], group)
        fresh_key = fresh_key * row_scales
        fresh_key = fresh_key * cosine + pltpu.roll(fresh_key, HEAD_SIZE // 2, 1) * sine
        fresh_key = fresh_key.astype(jnp.bfloat16).astype(jnp.float32)
        first = first + HEAD_SIZE
        fresh_value = spread(piece[:, first : first + HEAD_SIZE], group)
        fresh_value = (fresh_value * row_scales).astype(jnp.bfloat16).astype(jnp.float32)
        own = jnp.sum(query.astype(jnp.float32) * fresh_key, axis=1, keepdims=True) * scale
        scores = jnp.zeros((rows, slots), jnp.float32)
        for n in range(share):
            product = lax.dot_general(
                query,
                keys[n, :, lanes],
                (((1,), (1,)), ((), ())),
                preferred_element_type=jnp.float32,
            )
            scores = jnp.where(item == n, product, scores)
        scores = jnp.where(valid, scores * scale, -1e30)
        top = jnp.maximum(jnp.max(scores, axis=1, keepdims=True), own)
        weights = jnp.where(valid, jnp.exp(scores - top), 0.0)
        own_weight = jnp.exp(own - top)
        total = jnp.sum(weights, axis=1, keepdims=True) + own_weight
        mixed = own_weight.astype(jnp.bfloat16).astype(jnp.float32) * fresh_value
        for n in range(share):
            mixed = mixed + jnp.dot(
                jnp.where(item == n, weights, 0.0).astype(jnp.bfloat16),
                values[n, :, lanes],
                preferred_element_type=jnp.float32,
            )
        mixed = mixed / total
        outs[offset][...] = jnp.concatenate(
            [mixed[h * share : (h + 1) * share] for h in range(group)], axis=1
        ).astype(jnp.bfloat16)


def assemble_kernel(count, *refs):
    pieces = [refs[order(count).index(offset)] for offset in range(count)]
    out, held = refs[count], refs[count + 1]
    me = lax.axis_index("gy")
    for offset in range(count):
        held[me ^ offset] = pieces[offset][...].astype(jnp.float32)
    out[...] = jnp.concatenate([held[n] for n in range(count)], axis=0).astype(jnp.bfloat16)


def output_kernel(count, *refs):
    pieces = [refs[wide_order(count).index(offset)] for offset in range(count)]
    weights = refs[count : count + LOADS]
    outs, (held,) = refs[count + LOADS : 2 * count + LOADS], refs[2 * count + LOADS :]
    flip = lax.axis_index("gx") ^ lax.axis_index("gy")
    for offset in range(count):
        held[flip ^ offset] = pieces[offset][...]
    rows = held.shape[1]
    left = held[...].reshape(count * rows, held.shape[2])
    columns = weights[0].shape[1]
    step = min(columns, 512)
    for first in range(0, columns, step):
        product, start = 0.0, 0
        for weight in weights:
            depth = weight.shape[0]
            product = product + jnp.dot(
                left[:, start : start + depth],
                weight[:, first : first + step],
                preferred_element_type=jnp.float32,
            )
            start += depth
        product = product.astype(jnp.bfloat16)
        for offset in range(count):
            outs[offset][:, first : first + step] = product[offset * rows : (offset + 1) * rows]


def add_kernel(count, *refs):
    total = refs[0][...].astype(jnp.float32)
    for piece in refs[1:count]:
        total = total + piece[...].astype(jnp.float32)
    refs[count][...] = total.astype(jnp.bfloat16)


def rotary_kernel(share, lengths, cosines, sines, filled):
    rows = cosines.shape[0]
    item = lax.broadcasted_iota(jnp.int32, (rows, HEAD_SIZE), 0) % share
    column = lax.broadcasted_iota(jnp.int32, (rows, HEAD_SIZE), 1)
    half = HEAD_SIZE // 2
    length = jnp.zeros((rows, HEAD_SIZE), jnp.int32)
    for n in range(share):
        length = jnp.where(item == n, lengths[n], length)
    power = (column % half).astype(jnp.float32) * (2.0 / HEAD_SIZE)
    angles = length.astype(jnp.float32) * jnp.exp(-math.log(500000.0) * power)
    sine = jnp.sin(angles)
    cosines[...] = jnp.cos(angles)
    sines[...] = jnp.where(column < half, -sine, sine)
    filled[...] = length


def loading(kernel, loads, counts, *refs):
    inputs, outputs = counts
    many = len(loads)
    sources, refs = refs[:many], refs[many:]
    if many:
        targets, sems = refs[inputs + outputs : inputs + outputs + many], refs[-1]
        refs = refs[: inputs + outputs] + refs[inputs + outputs + many : -1]
    copies = [
        pltpu.make_async_copy(sources[n].at[pl.ds(first, rows)], targets[n], sems.at[n])
        for n, (first, rows) in enumerate(loads)
    ]
    for copy in copies:
        copy.start()
    if kernel is not None and copies:
        pl.when(lax.axis_index("gy") >= 0)(lambda: kernel(*refs))
    elif kernel is not None:
        kernel(*refs)
    for copy in copies:
        copy.wait()


def call(kernel, outs, scratch, args, name, limit, scalars=0, loads=(), flops=0):
    arrays = [pltpu.with_memory_space_constraint(load[0], pltpu.HBM) for load in loads]
    parts = [load[1:] for load in loads]
    size = sum(2 * rows * array.shape[1] for array, _, rows in loads)
    results = pl.pallas_call(
        functools.partial(loading, kernel, parts, (len(args), len(outs))),
        out_shape=[*outs, *(pltpu.VMEM((rows, a.shape[1]), a.dtype) for a, _, rows in loads)],
        in_specs=[pl.BlockSpec(memory_space=pltpu.HBM)] * len(loads)
        + [VMEM] * (len(args) - scalars)
        + [pl.BlockSpec(memory_space=pltpu.SMEM)] * scalars,
        out_specs=[VMEM] * (len(outs) + len(loads)),
        scratch_shapes=scratch
        + ([pltpu.SemaphoreType.DMA((len(loads),))] if loads else []),
        cost_estimate=pl.CostEstimate(
            flops=flops, bytes_accessed=2 * size + (1 << 16), transcendentals=0
        ),
        compiler_params=pltpu.CompilerParams(vmem_limit_bytes=limit << 20),
        name=name,
    )(*arrays, *args)
    return results[: len(outs)], results[len(outs) :]


def array(shape, dtype=jnp.bfloat16):
    return jax.ShapeDtypeStruct(shape, dtype)


def order(count):
    return [0, *range(count - 1, 0, -1)]


def wide_order(count):
    half = count // 2
    return [0, half, *range(count - 1, half, -1), *range(half - 1, 0, -1)]


def exchange(pieces, axis):
    count = len(pieces)
    result = list(pieces)
    for offset in range(count - 1, 0, -1):
        result[offset] = lax.ppermute(
            pieces[offset], axis, [(n, n ^ offset) for n in range(count)]
        )
    return result


def per_device(
    hidden_states,
    norm_gain,
    w_query,
    key_weight,
    value_weight,
    w_output,
    stored_key_cache,
    stored_value_cache,
    filled_lengths,
):
    across, down = lax.axis_size("gx"), lax.axis_size("gy")
    assert across == down and across & (across - 1) == 0
    count = down
    share, slots, cache_width = stored_key_cache.shape
    rows, depth = hidden_states.shape
    features = depth * across
    query_columns, key_columns = w_query.shape[1], key_weight.shape[1]
    kv_heads = cache_width // HEAD_SIZE
    group = query_columns * down // HEAD_SIZE // kv_heads

    used = query_columns + 2 * key_columns
    width = -(-used // LANES) * LANES + LANES
    out_rows, out_columns = w_output.shape
    cuts = [out_rows * cut // 8 for cut in CUTS]

    with jax.named_scope("gather_hidden"):
        gathered = exchange([hidden_states] * count, "gy")
    with jax.named_scope("fetch_query"):
        table = array((share * group, HEAD_SIZE), jnp.float32)
        (cosine, sine, filled), weights = call(
            functools.partial(rotary_kernel, share),
            [table, table, array(table.shape, jnp.int32)],
            [],
            [filled_lengths],
            "fetch_query",
            4,
            scalars=1,
            loads=[(w_query, 0, depth)],
        )
    with jax.named_scope("project"):
        partial, output_weights = call(
            functools.partial(project_kernel, count, width),
            [array((rows, width))] * count,
            [
                pltpu.VMEM((count, rows, depth), jnp.bfloat16),
                pltpu.VMEM((count, rows, LANES), jnp.float32),
            ],
            [
                *(gathered[k] for k in wide_order(count)),
                norm_gain,
                *weights,
                key_weight,
                value_weight,
            ],
            "project",
            8,
            loads=[(w_output, 0, cuts[0])],
            flops=2 * count * rows * depth * used,
        )
    with jax.named_scope("sum_gx"):
        received = exchange(partial, "gx")
        owned, _ = call(
            functools.partial(combine_kernel, count),
            [array((share, width))] * count,
            [pltpu.VMEM((count, share, width), jnp.float32)],
            [received[k] for k in wide_order(count)],
            "combine",
            4,
        )
    with jax.named_scope("to_owner"):
        owned = exchange(owned, "gy")

    with jax.named_scope("attend"):
        if key_columns == HEAD_SIZE:
            attended, _ = call(
                functools.partial(attend_kernel, count, group, features),
                [array((share, query_columns))] * count,
                [],
                [
                    *(owned[k] for k in order(count)),
                    stored_key_cache,
                    stored_value_cache,
                    cosine,
                    sine,
                    filled,
                ],
                "attend",
                8,
            )
        else:
            attended = attend_narrow(
                owned, used, features, stored_key_cache, stored_value_cache, cosine[:share],
                sine[:share], filled_lengths, query_columns, key_columns,
            )

    with jax.named_scope("to_head_rows"):
        attended = exchange(attended, "gy")
        (block,), _ = call(
            functools.partial(assemble_kernel, count),
            [array((count * share, query_columns))],
            [pltpu.VMEM((count, share, query_columns), jnp.float32)],
            [attended[k] for k in order(count)],
            "assemble",
            4,
        )
    with jax.named_scope("gather_gx"):
        blocks = exchange([block] * count, "gx")
        _, loaded = call(
            lambda *refs: None,
            [],
            [],
            [block],
            "fetch_output",
            4,
            loads=[(w_output, cuts[0], out_rows - cuts[0])],
        )
    with jax.named_scope("output"):
        products, _ = call(
            functools.partial(output_kernel, count),
            [array((count * share, out_columns))] * count,
            [pltpu.VMEM((count, count * share, query_columns), jnp.bfloat16)],
            [*(blocks[k] for k in wide_order(count)), *output_weights, *loaded],
            "output",
            8,
            flops=2 * count * count * share * out_rows * out_columns,
        )
    with jax.named_scope("sum_gy"):
        products = exchange(products, "gy")
        (result,), _ = call(
            functools.partial(add_kernel, count),
            [array((rows, out_columns))],
            [],
            [products[k] for k in wide_order(count)],
            "add",
            8,
        )
        return result


def attend_narrow(
    owned, used, features, key_rows, value_rows, cosine, sine, lengths, query_columns, key_columns
):
    count = len(owned)
    share, slots, cache_width = key_rows.shape
    kv_heads = cache_width // HEAD_SIZE
    group = query_columns * count // HEAD_SIZE // kv_heads
    me = lax.axis_index("gy")
    order = me ^ jnp.arange(count)
    stacked = jnp.stack(owned).astype(jnp.float32)
    squares = jnp.sum(stacked[0, :, -LANES:], axis=1)
    row_scale = lax.rsqrt(squares / features + EPSILON)[:, None]
    stacked = jnp.take(stacked, order, axis=0)

    def columns(first, size):
        block = stacked[:, :, first : first + size]
        return row_scale * block.transpose(1, 0, 2).reshape(share, count * size)

    def rotary(heads):
        swapped = jnp.concatenate(
            [heads[..., HEAD_SIZE // 2 :], heads[..., : HEAD_SIZE // 2]], axis=-1
        )
        shape = (share,) + (1,) * (heads.ndim - 2) + (HEAD_SIZE,)
        return (heads * cosine.reshape(shape) + swapped * sine.reshape(shape)).astype(jnp.bfloat16)

    query = rotary(columns(0, query_columns).reshape(share, kv_heads, group, HEAD_SIZE))
    fresh_key = rotary(
        columns(query_columns, key_columns).reshape(share, kv_heads, HEAD_SIZE)
    )
    fresh_value = columns(query_columns + key_columns, key_columns).astype(jnp.bfloat16)
    key_heads = key_rows.reshape(share, slots, kv_heads, HEAD_SIZE)
    value_heads = value_rows.reshape(share, slots, kv_heads, HEAD_SIZE)
    scale = 1.0 / HEAD_SIZE**0.5
    scores = scale * jnp.einsum(
        "nkgd,nlkd->nkgl", query, key_heads, preferred_element_type=jnp.float32
    )
    own = scale * jnp.einsum(
        "nkgd,nkd->nkg", query, fresh_key, preferred_element_type=jnp.float32
    )
    valid = jnp.arange(slots)[None, None, None, :] < lengths[:, None, None, None]
    scores = jnp.where(valid, scores, -1e30)
    top = jnp.maximum(jnp.max(scores, axis=-1), own)
    weights = jnp.where(valid, jnp.exp(scores - top[..., None]), 0.0)
    own_weight = jnp.exp(own - top)
    total = jnp.sum(weights, axis=-1) + own_weight
    mixed = jnp.einsum(
        "nkgl,nlkd->nkgd",
        weights.astype(jnp.bfloat16),
        value_heads,
        preferred_element_type=jnp.float32,
    )
    own_weight = own_weight.astype(jnp.bfloat16).astype(jnp.float32)
    mixed = mixed + own_weight[..., None] * fresh_value.reshape(
        share, kv_heads, 1, HEAD_SIZE
    ).astype(jnp.float32)
    mixed = (mixed / total[..., None]).astype(jnp.bfloat16)
    blocks = mixed.reshape(share, count, query_columns).transpose(1, 0, 2)
    blocks = jnp.take(blocks, order, axis=0)
    return [blocks[offset] for offset in range(count)]


def solution(mesh):
    placed = (
        P(("parts", "gy"), "gx"),
        P("gx"),
        P("gx", "gy"),
        P("gx", "gy"),
        P("gx", "gy"),
        P("gy", "gx"),
        P(("parts", "gx", "gy"), None, None),
        P(("parts", "gx", "gy"), None, None),
        P(("parts", "gx", "gy")),
    )
    return jax.shard_map(
        per_device, mesh=mesh, in_specs=placed, out_specs=P(("parts", "gy"), "gx"), check_vma=False
    )
```

```python
import functools
import math

import jax
import jax.numpy as jnp
from jax import lax
from jax.experimental import pallas as pl
from jax.experimental.pallas import tpu as pltpu
from jax.sharding import PartitionSpec as P

HEAD_SIZE = 128
LANES = 128
EPSILON = 1e-05
ORDERS = {"hidden": (2, 3, 1), "sum_gx": (2, 3, 1), "to_owner": (3, 2, 1), "to_head_rows": (3, 2, 1), "gather_gx": (2, 3, 1), "sum_gy": (2, 3, 1)}
CUTS = (0, 3, 5, 8)
LOADS = len(CUTS) - 1
VMEM = pl.BlockSpec(memory_space=pltpu.VMEM)


def square_lanes(total):
    high = total.astype(jnp.bfloat16).astype(jnp.float32)
    rest = total - high
    middle = rest.astype(jnp.bfloat16).astype(jnp.float32)
    lane = lax.broadcasted_iota(jnp.int32, (total.shape[0], LANES), 1)
    low = rest - middle
    return jnp.where(lane == 0, high, jnp.where(lane == 1, middle, jnp.where(lane == 2, low, 0.0)))


def padded(left):
    missing = -left.shape[0] % 128
    if not missing:
        return left
    return jnp.concatenate([left, jnp.zeros((missing, left.shape[1]), left.dtype)], axis=0)


def project_kernel(count, width, *refs):
    pieces = [refs[order("hidden", count).index(offset)] for offset in range(count)]
    gain, w_query, key_weight, value_weight = refs[count : count + 4]
    outs, (held,) = refs[count + 4 : 2 * count + 4], refs[2 * count + 4 :]
    flip = lax.axis_index("gx") ^ lax.axis_index("gy") ^ 1
    gains = gain[...].astype(jnp.float32)[None, :]
    rows = pieces[0].shape[0]
    scaled = []
    for offset in range(count):
        states = pieces[offset][...].astype(jnp.float32)
        scaled.append((states * gains).astype(jnp.bfloat16))
        held[flip ^ offset, :, width - LANES :] = square_lanes(
            jnp.sum(states * states, axis=1, keepdims=True)
        ).astype(jnp.bfloat16)
    left = padded(jnp.concatenate(scaled, axis=0))
    start = 0
    for weight in (w_query, key_weight, value_weight):
        columns = weight.shape[1]
        step = min(columns, 512)
        for first in range(0, columns, step):
            product = jnp.dot(
                left, weight[:, first : first + step], preferred_element_type=jnp.float32
            ).astype(jnp.bfloat16)
            for offset in range(count):
                held[flip ^ offset, :, start : start + step] = product[
                    offset * rows : (offset + 1) * rows
                ]
            start += step
    for offset in range(count):
        outs[offset][...] = held[offset]
        if start < width - LANES:
            outs[offset][:, start : width - LANES] = jnp.zeros(
                (rows, width - LANES - start), jnp.bfloat16
            )


def combine_kernel(count, *refs):
    pieces = [refs[order("sum_gx", count).index(offset)] for offset in range(count)]
    outs, (held,) = refs[count : 2 * count], refs[2 * count :]
    total = pieces[0][...].astype(jnp.float32)
    for piece in pieces[1:]:
        total = total + piece[...].astype(jnp.float32)
    share = held.shape[1]
    width = total.shape[1]
    squares = square_lanes(jnp.sum(total[:, width - LANES :], axis=1, keepdims=True))
    for owner in range(count):
        rows = slice(owner * share, (owner + 1) * share)
        held[owner, :, : width - LANES] = total[rows, : width - LANES]
        held[owner, :, width - LANES :] = squares[rows]
    me = lax.axis_index("gy")
    for offset in range(count):
        outs[offset][...] = held[me ^ offset].astype(jnp.bfloat16)


def spread(rows, group):
    repeat = min(group, max(1, 8 // rows.shape[0]))
    tile = jnp.concatenate([rows] * repeat, axis=0) if repeat > 1 else rows
    wide = jnp.broadcast_to(tile[None], (group // repeat, *tile.shape))
    return wide.reshape(group * rows.shape[0], rows.shape[1])


def attend_kernel(count, group, features, *refs):
    pieces = [refs[order("to_owner", count).index(offset)] for offset in range(count)]
    keys, values, cosines, sines, filled = refs[count : count + 5]
    outs = refs[count + 5 :]
    share, slots = keys.shape[0], keys.shape[1]
    rows = share * group
    scale = 1.0 / HEAD_SIZE**0.5
    width = pieces[0].shape[1]
    me = lax.axis_index("gy")
    cosine, sine = cosines[...], sines[...]
    squares = jnp.sum(
        pieces[0][:, width - LANES :].astype(jnp.float32), axis=1, keepdims=True
    )
    row_scale = lax.rsqrt(squares / features + EPSILON)
    row_scales = spread(row_scale, group)
    item = lax.broadcasted_iota(jnp.int32, (rows, 1), 0) % share
    valid = lax.broadcasted_iota(jnp.int32, (rows, slots), 1) < filled[:, :1]
    states, scores = [], []
    for offset in range(count):
        piece = pieces[offset][...].astype(jnp.float32)
        head = me ^ offset
        lanes = pl.ds(pl.multiple_of(head * HEAD_SIZE, HEAD_SIZE), HEAD_SIZE)
        query = jnp.concatenate(
            [piece[:, h * HEAD_SIZE : (h + 1) * HEAD_SIZE] for h in range(group)], axis=0
        )
        query = query * row_scales
        query = query * cosine + pltpu.roll(query, HEAD_SIZE // 2, 1) * sine
        query = query.astype(jnp.bfloat16)
        first = group * HEAD_SIZE
        fresh_key = spread(piece[:, first : first + HEAD_SIZE], group) * row_scales
        fresh_key = fresh_key * cosine + pltpu.roll(fresh_key, HEAD_SIZE // 2, 1) * sine
        fresh_key = fresh_key.astype(jnp.bfloat16).astype(jnp.float32)
        first = first + HEAD_SIZE
        fresh_value = spread(piece[:, first : first + HEAD_SIZE], group) * row_scales
        fresh_value = fresh_value.astype(jnp.bfloat16).astype(jnp.float32)
        own = jnp.sum(query.astype(jnp.float32) * fresh_key, axis=1, keepdims=True) * scale
        states.append((lanes, own, fresh_value))
        products = [
            lax.dot_general(
                query,
                keys[n, :, lanes],
                (((1,), (1,)), ((), ())),
                preferred_element_type=jnp.float32,
            )
            for n in range(share)
        ]
        score = products[0]
        for n in range(1, share):
            score = jnp.where(item == n, products[n], score)
        scores.append(jnp.where(valid, score * scale, -1e30))
    tops = [
        jnp.maximum(jnp.max(score, axis=1, keepdims=True), own)
        for score, (_, own, _) in zip(scores, states)
    ]
    weights = [
        jnp.where(valid, jnp.exp(score - top), 0.0) for score, top in zip(scores, tops)
    ]
    for offset, (lanes, own, fresh_value) in enumerate(states):
        own_weight = jnp.exp(own - tops[offset])
        total = jnp.sum(weights[offset], axis=1, keepdims=True) + own_weight
        mixed = own_weight.astype(jnp.bfloat16).astype(jnp.float32) * fresh_value
        for n in range(share):
            mixed = mixed + jnp.dot(
                jnp.where(item == n, weights[offset], 0.0).astype(jnp.bfloat16),
                values[n, :, lanes],
                preferred_element_type=jnp.float32,
            )
        mixed = mixed / total
        outs[offset][...] = jnp.concatenate(
            [mixed[h * share : (h + 1) * share] for h in range(group)], axis=1
        ).astype(jnp.bfloat16)


def assemble_kernel(count, *refs):
    pieces = [refs[order("to_head_rows", count).index(offset)] for offset in range(count)]
    out, held = refs[count], refs[count + 1]
    me = lax.axis_index("gy")
    for offset in range(count):
        held[me ^ offset] = pieces[offset][...].astype(jnp.float32)
    out[...] = jnp.concatenate([held[n] for n in range(count)], axis=0).astype(jnp.bfloat16)


def output_kernel(count, *refs):
    pieces = [refs[order("gather_gx", count).index(offset)] for offset in range(count)]
    weights = refs[count : count + LOADS]
    outs, (held,) = refs[count + LOADS : 2 * count + LOADS], refs[2 * count + LOADS :]
    flip = lax.axis_index("gx") ^ lax.axis_index("gy") ^ 1
    for offset in range(count):
        held[flip ^ offset] = pieces[offset][...]
    rows = held.shape[1]
    left = padded(held[...].reshape(count * rows, held.shape[2]))
    columns = weights[0].shape[1]
    step = min(columns, 512)
    for first in range(0, columns, step):
        product, start = 0.0, 0
        for weight in weights:
            depth = weight.shape[0]
            product = product + jnp.dot(
                left[:, start : start + depth],
                weight[:, first : first + step],
                preferred_element_type=jnp.float32,
            )
            start += depth
        product = product.astype(jnp.bfloat16)
        for offset in range(count):
            outs[offset][:, first : first + step] = product[offset * rows : (offset + 1) * rows]


def add_kernel(count, *refs):
    total = refs[0][...].astype(jnp.float32)
    for piece in refs[1:count]:
        total = total + piece[...].astype(jnp.float32)
    refs[count][...] = total.astype(jnp.bfloat16)


def rotary_kernel(share, lengths, cosines, sines, filled):
    rows = cosines.shape[0]
    item = lax.broadcasted_iota(jnp.int32, (rows, HEAD_SIZE), 0) % share
    column = lax.broadcasted_iota(jnp.int32, (rows, HEAD_SIZE), 1)
    half = HEAD_SIZE // 2
    length = jnp.zeros((rows, HEAD_SIZE), jnp.int32)
    for n in range(share):
        length = jnp.where(item == n, lengths[n], length)
    power = (column % half).astype(jnp.float32) * (2.0 / HEAD_SIZE)
    angles = length.astype(jnp.float32) * jnp.exp(-math.log(500000.0) * power)
    sine = jnp.sin(angles)
    cosines[...] = jnp.cos(angles)
    sines[...] = jnp.where(column < half, -sine, sine)
    filled[...] = length


def loading(kernel, loads, counts, *refs):
    skip, inputs, outputs = counts
    many = len(loads)
    sources, refs = refs[:many], refs[many + skip :]
    if many:
        targets, sems = refs[inputs + outputs : inputs + outputs + many], refs[-1]
        refs = refs[: inputs + outputs] + refs[inputs + outputs + many : -1]
    copies = [
        pltpu.make_async_copy(sources[n].at[pl.ds(first, rows)], targets[n], sems.at[n])
        for n, (first, rows) in enumerate(loads)
    ]
    for copy in copies:
        copy.start()
    if kernel is not None and copies:
        pl.when(lax.axis_index("gy") >= 0)(lambda: kernel(*refs))
    elif kernel is not None:
        kernel(*refs)
    for copy in copies:
        copy.wait()


def call(kernel, outs, scratch, args, name, limit, scalars=0, loads=(), flops=0, after=()):
    arrays = [pltpu.with_memory_space_constraint(load[0], pltpu.HBM) for load in loads]
    parts = [load[1:] for load in loads]
    size = sum(2 * rows * array.shape[1] for array, _, rows in loads)
    results = pl.pallas_call(
        functools.partial(loading, kernel, parts, (len(after), len(args), len(outs))),
        out_shape=[*outs, *(pltpu.VMEM((rows, a.shape[1]), a.dtype) for a, _, rows in loads)],
        in_specs=[pl.BlockSpec(memory_space=pltpu.HBM)] * len(loads)
        + [pl.BlockSpec(memory_space=pl.ANY)] * len(after)
        + [VMEM] * (len(args) - scalars)
        + [pl.BlockSpec(memory_space=pltpu.SMEM)] * scalars,
        out_specs=[VMEM] * (len(outs) + len(loads)),
        scratch_shapes=scratch
        + ([pltpu.SemaphoreType.DMA((len(loads),))] if loads else []),
        cost_estimate=pl.CostEstimate(
            flops=flops, bytes_accessed=2 * size + (1 << 16), transcendentals=0
        ),
        compiler_params=pltpu.CompilerParams(vmem_limit_bytes=limit << 20),
        name=name,
    )(*arrays, *after, *args)
    return results[: len(outs)], results[len(outs) :]


def array(shape, dtype=jnp.bfloat16):
    return jax.ShapeDtypeStruct(shape, dtype)


def order(name, count):
    if count == len(ORDERS[name]) + 1:
        return (0, *ORDERS[name])
    return (0, *range(count - 1, 0, -1))


def exchange(pieces, axis, name):
    count = len(pieces)
    result = list(pieces)
    for offset in order(name, count)[1:]:
        result[offset] = lax.ppermute(
            pieces[offset], axis, [(n, n ^ offset) for n in range(count)]
        )
    return result


def crossing_exchange(pieces, name):
    count = len(pieces)
    result = list(pieces)
    for offset in (*order(name, count)[1:], 0):
        result[offset] = lax.ppermute(
            pieces[offset],
            ("gx", "gy"),
            [(n, (n ^ count) ^ offset) for n in range(lax.axis_size("gx") * count)],
        )
    return result


def per_device(
    hidden_states,
    norm_gain,
    w_query,
    key_weight,
    value_weight,
    w_output,
    stored_key_cache,
    stored_value_cache,
    filled_lengths,
):
    across, down = lax.axis_size("gx"), lax.axis_size("gy")
    assert across == down and across & (across - 1) == 0
    count = down
    share, slots, cache_width = stored_key_cache.shape
    rows, depth = hidden_states.shape
    features = depth * across
    query_columns, key_columns = w_query.shape[1], key_weight.shape[1]
    kv_heads = cache_width // HEAD_SIZE
    group = query_columns * down // HEAD_SIZE // kv_heads

    used = query_columns + 2 * key_columns
    width = -(-used // LANES) * LANES + LANES
    out_rows, out_columns = w_output.shape
    cuts = [out_rows * cut // 8 for cut in CUTS]

    def fetch(name, index, after):
        first, last = cuts[index : index + 2]
        return call(None, [], [], [], name, 4, loads=[(w_output, first, last - first)], after=[after])[1]

    with jax.named_scope("gather_hidden"):
        gathered = exchange([hidden_states] * count, "gy", "hidden")
    with jax.named_scope("fetch_query"):
        table = array((share * group, HEAD_SIZE), jnp.float32)
        (cosine, sine, filled), weights = call(
            functools.partial(rotary_kernel, share),
            [table, table, array(table.shape, jnp.int32)],
            [],
            [filled_lengths],
            "fetch_query",
            4,
            scalars=1,
            loads=[(w_query, 0, depth)],
        )
    with jax.named_scope("project"):
        partial, output_weights = call(
            functools.partial(project_kernel, count, width),
            [array((rows, width))] * count,
            [pltpu.VMEM((count, rows, width), jnp.bfloat16)],
            [
                *(gathered[k] for k in order("hidden", count)),
                norm_gain,
                *weights,
                key_weight,
                value_weight,
            ],
            "project",
            8,
            loads=[(w_output, cuts[0], cuts[1] - cuts[0])],
            flops=2 * count * rows * depth * used,
        )
    with jax.named_scope("sum_gx"):
        received = exchange(partial, "gx", "sum_gx")
        output_weights += fetch("fetch_output", 1, partial[0])
        owned, _ = call(
            functools.partial(combine_kernel, count),
            [array((share, width))] * count,
            [pltpu.VMEM((count, share, width), jnp.float32)],
            [received[k] for k in order("sum_gx", count)],
            "combine",
            4,
            after=output_weights[1:],
        )
    with jax.named_scope("to_owner"):
        owned = crossing_exchange(owned, "to_owner")

    with jax.named_scope("attend"):
        if key_columns == HEAD_SIZE:
            attended, _ = call(
                functools.partial(attend_kernel, count, group, features),
                [array((share, query_columns))] * count,
                [],
                [
                    *(owned[k] for k in order("to_owner", count)),
                    stored_key_cache,
                    stored_value_cache,
                    cosine,
                    sine,
                    filled,
                ],
                "attend",
                8,
            )
        else:
            attended = attend_narrow(
                owned, used, features, stored_key_cache, stored_value_cache, cosine[:share],
                sine[:share], filled_lengths, query_columns, key_columns,
            )

    with jax.named_scope("to_head_rows"):
        attended = crossing_exchange(attended, "to_head_rows")
        (block,), _ = call(
            functools.partial(assemble_kernel, count),
            [array((count * share, query_columns))],
            [pltpu.VMEM((count, share, query_columns), jnp.float32)],
            [attended[k] for k in order("to_head_rows", count)],
            "assemble",
            4,
        )
    with jax.named_scope("gather_gx"):
        blocks = exchange([block] * count, "gx", "gather_gx")
        output_weights += fetch("fetch_output", 2, block)
    with jax.named_scope("output"):
        products, _ = call(
            functools.partial(output_kernel, count),
            [array((count * share, out_columns))] * count,
            [pltpu.VMEM((count, count * share, query_columns), jnp.bfloat16)],
            [*(blocks[k] for k in order("gather_gx", count)), *output_weights],
            "output",
            8,
            flops=2 * count * count * share * out_rows * out_columns,
        )
    with jax.named_scope("sum_gy"):
        products = exchange(products, "gy", "sum_gy")
        (result,), _ = call(
            functools.partial(add_kernel, count),
            [array((rows, out_columns))],
            [],
            [products[k] for k in order("sum_gy", count)],
            "add",
            8,
        )
        return result


def attend_narrow(
    owned, used, features, key_rows, value_rows, cosine, sine, lengths, query_columns, key_columns
):
    count = len(owned)
    share, slots, cache_width = key_rows.shape
    kv_heads = cache_width // HEAD_SIZE
    group = query_columns * count // HEAD_SIZE // kv_heads
    me = lax.axis_index("gy")
    order = me ^ jnp.arange(count)
    stacked = jnp.stack(owned).astype(jnp.float32)
    squares = jnp.sum(stacked[0, :, -LANES:], axis=1)
    row_scale = lax.rsqrt(squares / features + EPSILON)[:, None]
    stacked = jnp.take(stacked, order, axis=0)

    def columns(first, size):
        block = stacked[:, :, first : first + size]
        return row_scale * block.transpose(1, 0, 2).reshape(share, count * size)

    def rotary(heads):
        swapped = jnp.concatenate(
            [heads[..., HEAD_SIZE // 2 :], heads[..., : HEAD_SIZE // 2]], axis=-1
        )
        shape = (share,) + (1,) * (heads.ndim - 2) + (HEAD_SIZE,)
        return (heads * cosine.reshape(shape) + swapped * sine.reshape(shape)).astype(jnp.bfloat16)

    query = rotary(columns(0, query_columns).reshape(share, kv_heads, group, HEAD_SIZE))
    fresh_key = rotary(
        columns(query_columns, key_columns).reshape(share, kv_heads, HEAD_SIZE)
    )
    fresh_value = columns(query_columns + key_columns, key_columns).astype(jnp.bfloat16)
    key_heads = key_rows.reshape(share, slots, kv_heads, HEAD_SIZE)
    value_heads = value_rows.reshape(share, slots, kv_heads, HEAD_SIZE)
    scale = 1.0 / HEAD_SIZE**0.5
    scores = scale * jnp.einsum(
        "nkgd,nlkd->nkgl", query, key_heads, preferred_element_type=jnp.float32
    )
    own = scale * jnp.einsum(
        "nkgd,nkd->nkg", query, fresh_key, preferred_element_type=jnp.float32
    )
    valid = jnp.arange(slots)[None, None, None, :] < lengths[:, None, None, None]
    scores = jnp.where(valid, scores, -1e30)
    top = jnp.maximum(jnp.max(scores, axis=-1), own)
    weights = jnp.where(valid, jnp.exp(scores - top[..., None]), 0.0)
    own_weight = jnp.exp(own - top)
    total = jnp.sum(weights, axis=-1) + own_weight
    mixed = jnp.einsum(
        "nkgl,nlkd->nkgd",
        weights.astype(jnp.bfloat16),
        value_heads,
        preferred_element_type=jnp.float32,
    )
    own_weight = own_weight.astype(jnp.bfloat16).astype(jnp.float32)
    mixed = mixed + own_weight[..., None] * fresh_value.reshape(
        share, kv_heads, 1, HEAD_SIZE
    ).astype(jnp.float32)
    mixed = (mixed / total[..., None]).astype(jnp.bfloat16)
    blocks = mixed.reshape(share, count, query_columns).transpose(1, 0, 2)
    blocks = jnp.take(blocks, order, axis=0)
    return [blocks[offset] for offset in range(count)]


def solution(mesh):
    placed = (
        P(("parts", "gy"), "gx"),
        P("gx"),
        P("gx", "gy"),
        P("gx", "gy"),
        P("gx", "gy"),
        P("gy", "gx"),
        P(("parts", "gx", "gy"), None, None),
        P(("parts", "gx", "gy"), None, None),
        P(("parts", "gx", "gy")),
    )
    return jax.shard_map(
        per_device, mesh=mesh, in_specs=placed, out_specs=P(("parts", "gy"), "gx"), check_vma=False
    )
```

```python
import functools
import math

import jax
import jax.numpy as jnp
from jax import lax
from jax.experimental import pallas as pl
from jax.experimental.pallas import tpu as pltpu
from jax.sharding import PartitionSpec as P

HEAD_SIZE = 128
LANES = 128
EPSILON = 1e-05
ORDERS = {
    "hidden": (2, 3, 1),
    "sum_gx": (2, 1, 3),
    "to_owner": (2, 3, 1),
    "to_head_rows": (2, 3, 1),
    "gather_gx": (2, 1, 3),
    "sum_gy": (2, 1, 3),
}
CUTS = (0, 3, 5, 8)
LOADS = len(CUTS) - 1
VMEM = pl.BlockSpec(memory_space=pltpu.VMEM)


def square_lanes(total):
    high = total.astype(jnp.bfloat16).astype(jnp.float32)
    rest = total - high
    middle = rest.astype(jnp.bfloat16).astype(jnp.float32)
    lane = lax.broadcasted_iota(jnp.int32, (total.shape[0], LANES), 1)
    low = rest - middle
    return jnp.where(lane == 0, high, jnp.where(lane == 1, middle, jnp.where(lane == 2, low, 0.0)))


def padded(left):
    missing = -left.shape[0] % 128
    if not missing:
        return left
    return jnp.concatenate([left, jnp.zeros((missing, left.shape[1]), left.dtype)], axis=0)


def project_kernel(count, width, *refs):
    pieces = [refs[order("hidden", count).index(offset)] for offset in range(count)]
    gain, w_query, key_weight, value_weight = refs[count : count + 4]
    outs, (held,) = refs[count + 4 : 2 * count + 4], refs[2 * count + 4 :]
    flip = lax.axis_index("gx") ^ lax.axis_index("gy") ^ 1
    gains = gain[...].astype(jnp.float32)[None, :]
    rows = pieces[0].shape[0]
    scaled = []
    for offset in range(count):
        states = pieces[offset][...].astype(jnp.float32)
        scaled.append((states * gains).astype(jnp.bfloat16))
        held[flip ^ offset, :, width - LANES :] = square_lanes(
            jnp.sum(states * states, axis=1, keepdims=True)
        ).astype(jnp.bfloat16)
    left = padded(jnp.concatenate(scaled, axis=0))
    start = 0
    for weight in (w_query, key_weight, value_weight):
        columns = weight.shape[1]
        step = min(columns, 512)
        for first in range(0, columns, step):
            product = jnp.dot(
                left, weight[:, first : first + step], preferred_element_type=jnp.float32
            ).astype(jnp.bfloat16)
            for offset in range(count):
                held[flip ^ offset, :, start : start + step] = product[
                    offset * rows : (offset + 1) * rows
                ]
            start += step
    for offset in range(count):
        outs[offset][...] = held[offset]
        if start < width - LANES:
            outs[offset][:, start : width - LANES] = jnp.zeros(
                (rows, width - LANES - start), jnp.bfloat16
            )


def combine_kernel(count, *refs):
    pieces = [refs[order("sum_gx", count).index(offset)] for offset in range(count)]
    outs, (held,) = refs[count : 2 * count], refs[2 * count :]
    total = pieces[0][...].astype(jnp.float32)
    for piece in pieces[1:]:
        total = total + piece[...].astype(jnp.float32)
    share = held.shape[1]
    width = total.shape[1]
    squares = square_lanes(jnp.sum(total[:, width - LANES :], axis=1, keepdims=True))
    for owner in range(count):
        rows = slice(owner * share, (owner + 1) * share)
        held[owner, :, : width - LANES] = total[rows, : width - LANES]
        held[owner, :, width - LANES :] = squares[rows]
    me = lax.axis_index("gy")
    for offset in range(count):
        outs[offset][...] = held[me ^ offset].astype(jnp.bfloat16)


def spread(rows, group):
    repeat = min(group, max(1, 8 // rows.shape[0]))
    tile = jnp.concatenate([rows] * repeat, axis=0) if repeat > 1 else rows
    wide = jnp.broadcast_to(tile[None], (group // repeat, *tile.shape))
    return wide.reshape(group * rows.shape[0], rows.shape[1])


def attend_kernel(count, group, features, *refs):
    pieces = [refs[order("to_owner", count).index(offset)] for offset in range(count)]
    keys, values, cosines, sines, filled = refs[count : count + 5]
    outs = refs[count + 5 :]
    share, slots = keys.shape[0], keys.shape[1]
    rows = share * group
    scale = 1.0 / HEAD_SIZE**0.5
    width = pieces[0].shape[1]
    me = lax.axis_index("gy")
    cosine, sine = cosines[...], sines[...]
    squares = jnp.sum(
        pieces[0][:, width - LANES :].astype(jnp.float32), axis=1, keepdims=True
    )
    row_scale = lax.rsqrt(squares / features + EPSILON)
    row_scales = spread(row_scale, group)
    item = lax.broadcasted_iota(jnp.int32, (rows, 1), 0) % share
    valid = lax.broadcasted_iota(jnp.int32, (rows, slots), 1) < filled[:, :1]
    states, scores = [], []
    for offset in range(count):
        piece = pieces[offset][...].astype(jnp.float32)
        head = me ^ offset
        lanes = pl.ds(pl.multiple_of(head * HEAD_SIZE, HEAD_SIZE), HEAD_SIZE)
        query = jnp.concatenate(
            [piece[:, h * HEAD_SIZE : (h + 1) * HEAD_SIZE] for h in range(group)], axis=0
        )
        query = query * row_scales
        query = query * cosine + pltpu.roll(query, HEAD_SIZE // 2, 1) * sine
        query = query.astype(jnp.bfloat16)
        first = group * HEAD_SIZE
        fresh_key = spread(piece[:, first : first + HEAD_SIZE], group) * row_scales
        fresh_key = fresh_key * cosine + pltpu.roll(fresh_key, HEAD_SIZE // 2, 1) * sine
        fresh_key = fresh_key.astype(jnp.bfloat16).astype(jnp.float32)
        first = first + HEAD_SIZE
        fresh_value = spread(piece[:, first : first + HEAD_SIZE], group) * row_scales
        fresh_value = fresh_value.astype(jnp.bfloat16).astype(jnp.float32)
        own = jnp.sum(query.astype(jnp.float32) * fresh_key, axis=1, keepdims=True) * scale
        states.append((lanes, own, fresh_value))
        products = [
            lax.dot_general(
                query,
                keys[n, :, lanes],
                (((1,), (1,)), ((), ())),
                preferred_element_type=jnp.float32,
            )
            for n in range(share)
        ]
        score = products[0]
        for n in range(1, share):
            score = jnp.where(item == n, products[n], score)
        scores.append(jnp.where(valid, score * scale, -1e30))
    tops = [
        jnp.maximum(jnp.max(score, axis=1, keepdims=True), own)
        for score, (_, own, _) in zip(scores, states)
    ]
    weights = [
        jnp.where(valid, jnp.exp(score - top), 0.0) for score, top in zip(scores, tops)
    ]
    for offset, (lanes, own, fresh_value) in enumerate(states):
        own_weight = jnp.exp(own - tops[offset])
        total = jnp.sum(weights[offset], axis=1, keepdims=True) + own_weight
        mixed = own_weight.astype(jnp.bfloat16).astype(jnp.float32) * fresh_value
        for n in range(share):
            mixed = mixed + jnp.dot(
                jnp.where(item == n, weights[offset], 0.0).astype(jnp.bfloat16),
                values[n, :, lanes],
                preferred_element_type=jnp.float32,
            )
        mixed = mixed / total
        outs[offset][...] = jnp.concatenate(
            [mixed[h * share : (h + 1) * share] for h in range(group)], axis=1
        ).astype(jnp.bfloat16)


def assemble_kernel(count, *refs):
    pieces = [refs[order("to_head_rows", count).index(offset)] for offset in range(count)]
    out, held = refs[count], refs[count + 1]
    me = lax.axis_index("gy")
    for offset in range(count):
        held[me ^ offset] = pieces[offset][...].astype(jnp.float32)
    out[...] = jnp.concatenate([held[n] for n in range(count)], axis=0).astype(jnp.bfloat16)


def output_kernel(count, *refs):
    pieces = [refs[order("gather_gx", count).index(offset)] for offset in range(count)]
    weights = refs[count : count + LOADS]
    outs, (held,) = refs[count + LOADS : 2 * count + LOADS], refs[2 * count + LOADS :]
    flip = lax.axis_index("gx") ^ lax.axis_index("gy") ^ 1
    for offset in range(count):
        held[flip ^ offset] = pieces[offset][...]
    rows = held.shape[1]
    left = padded(held[...].reshape(count * rows, held.shape[2]))
    columns = weights[0].shape[1]
    step = min(columns, 512)
    for first in range(0, columns, step):
        product, start = 0.0, 0
        for weight in weights:
            depth = weight.shape[0]
            product = product + jnp.dot(
                left[:, start : start + depth],
                weight[:, first : first + step],
                preferred_element_type=jnp.float32,
            )
            start += depth
        product = product.astype(jnp.bfloat16)
        for offset in range(count):
            outs[offset][:, first : first + step] = product[offset * rows : (offset + 1) * rows]


def add_kernel(count, *refs):
    total = refs[0][...].astype(jnp.float32)
    for piece in refs[1:count]:
        total = total + piece[...].astype(jnp.float32)
    refs[count][...] = total.astype(jnp.bfloat16)


def rotary_kernel(share, lengths, cosines, sines, filled):
    rows = cosines.shape[0]
    item = lax.broadcasted_iota(jnp.int32, (rows, HEAD_SIZE), 0) % share
    column = lax.broadcasted_iota(jnp.int32, (rows, HEAD_SIZE), 1)
    half = HEAD_SIZE // 2
    length = jnp.zeros((rows, HEAD_SIZE), jnp.int32)
    for n in range(share):
        length = jnp.where(item == n, lengths[n], length)
    power = (column % half).astype(jnp.float32) * (2.0 / HEAD_SIZE)
    angles = length.astype(jnp.float32) * jnp.exp(-math.log(500000.0) * power)
    sine = jnp.sin(angles)
    cosines[...] = jnp.cos(angles)
    sines[...] = jnp.where(column < half, -sine, sine)
    filled[...] = length


def loading(kernel, loads, counts, *refs):
    skip, inputs, outputs = counts
    many = len(loads)
    sources, refs = refs[:many], refs[many + skip :]
    if many:
        targets, sems = refs[inputs + outputs : inputs + outputs + many], refs[-1]
        refs = refs[: inputs + outputs] + refs[inputs + outputs + many : -1]
    copies = [
        pltpu.make_async_copy(sources[n].at[pl.ds(first, rows)], targets[n], sems.at[n])
        for n, (first, rows) in enumerate(loads)
    ]
    for copy in copies:
        copy.start()
    if kernel is not None and copies:
        pl.when(lax.axis_index("gy") >= 0)(lambda: kernel(*refs))
    elif kernel is not None:
        kernel(*refs)
    for copy in copies:
        copy.wait()


def call(kernel, outs, scratch, args, name, limit, scalars=0, loads=(), flops=0, after=()):
    arrays = [pltpu.with_memory_space_constraint(load[0], pltpu.HBM) for load in loads]
    parts = [load[1:] for load in loads]
    size = sum(2 * rows * array.shape[1] for array, _, rows in loads)
    results = pl.pallas_call(
        functools.partial(loading, kernel, parts, (len(after), len(args), len(outs))),
        out_shape=[*outs, *(pltpu.VMEM((rows, a.shape[1]), a.dtype) for a, _, rows in loads)],
        in_specs=[pl.BlockSpec(memory_space=pltpu.HBM)] * len(loads)
        + [pl.BlockSpec(memory_space=pl.ANY)] * len(after)
        + [VMEM] * (len(args) - scalars)
        + [pl.BlockSpec(memory_space=pltpu.SMEM)] * scalars,
        out_specs=[VMEM] * (len(outs) + len(loads)),
        scratch_shapes=scratch
        + ([pltpu.SemaphoreType.DMA((len(loads),))] if loads else []),
        cost_estimate=pl.CostEstimate(
            flops=flops, bytes_accessed=2 * size + (1 << 16), transcendentals=0
        ),
        compiler_params=pltpu.CompilerParams(vmem_limit_bytes=limit << 20),
        name=name,
    )(*arrays, *after, *args)
    return results[: len(outs)], results[len(outs) :]


def array(shape, dtype=jnp.bfloat16):
    return jax.ShapeDtypeStruct(shape, dtype)


def order(name, count):
    if count == len(ORDERS[name]) + 1:
        return (0, *ORDERS[name])
    return (0, *range(count - 1, 0, -1))


def exchange(pieces, axis, name):
    count = len(pieces)
    result = list(pieces)
    for offset in order(name, count)[1:]:
        result[offset] = lax.ppermute(
            pieces[offset], axis, [(n, n ^ offset) for n in range(count)]
        )
    return result


def crossing_exchange(pieces, name):
    count = len(pieces)
    result = list(pieces)
    for offset in (*order(name, count)[1:], 0):
        result[offset] = lax.ppermute(
            pieces[offset],
            ("gx", "gy"),
            [(n, (n ^ count) ^ offset) for n in range(lax.axis_size("gx") * count)],
        )
    return result


def per_device(
    hidden_states,
    norm_gain,
    w_query,
    key_weight,
    value_weight,
    w_output,
    stored_key_cache,
    stored_value_cache,
    filled_lengths,
):
    across, down = lax.axis_size("gx"), lax.axis_size("gy")
    assert across == down and across & (across - 1) == 0
    count = down
    share, slots, cache_width = stored_key_cache.shape
    rows, depth = hidden_states.shape
    features = depth * across
    query_columns, key_columns = w_query.shape[1], key_weight.shape[1]
    kv_heads = cache_width // HEAD_SIZE
    group = query_columns * down // HEAD_SIZE // kv_heads

    used = query_columns + 2 * key_columns
    width = -(-used // LANES) * LANES + LANES
    out_rows, out_columns = w_output.shape
    cuts = [out_rows * cut // 8 for cut in CUTS]

    def load(index):
        return w_output, cuts[index], cuts[index + 1] - cuts[index]

    with jax.named_scope("gather_hidden"):
        gathered = exchange([hidden_states] * count, "gy", "hidden")
    with jax.named_scope("fetch_query"):
        _, weights = call(None, [], [], [], "fetch_query", 4, loads=[(w_query, 0, depth)])
    with jax.named_scope("project"):
        partial, output_weights = call(
            functools.partial(project_kernel, count, width),
            [array((rows, width))] * count,
            [pltpu.VMEM((count, rows, width), jnp.bfloat16)],
            [
                *(gathered[k] for k in order("hidden", count)),
                norm_gain,
                *weights,
                key_weight,
                value_weight,
            ],
            "project",
            8,
            loads=[load(0)],
            flops=2 * count * rows * depth * used,
        )
    with jax.named_scope("sum_gx"):
        received = exchange(partial, "gx", "sum_gx")
        table = array((share * group, HEAD_SIZE), jnp.float32)
        (cosine, sine, filled), loaded = call(
            functools.partial(rotary_kernel, share),
            [table, table, array(table.shape, jnp.int32)],
            [],
            [filled_lengths],
            "fetch_output",
            4,
            scalars=1,
            loads=[load(1)],
            after=partial[:1],
        )
        output_weights += loaded
        owned, _ = call(
            functools.partial(combine_kernel, count),
            [array((share, width))] * count,
            [pltpu.VMEM((count, share, width), jnp.float32)],
            [received[k] for k in order("sum_gx", count)],
            "combine",
            4,
            after=output_weights[1:],
        )
    with jax.named_scope("to_owner"):
        owned = crossing_exchange(owned, "to_owner")

    with jax.named_scope("attend"):
        if key_columns == HEAD_SIZE:
            attended, _ = call(
                functools.partial(attend_kernel, count, group, features),
                [array((share, query_columns))] * count,
                [],
                [
                    *(owned[k] for k in order("to_owner", count)),
                    stored_key_cache,
                    stored_value_cache,
                    cosine,
                    sine,
                    filled,
                ],
                "attend",
                8,
            )
        else:
            attended = attend_narrow(
                owned, used, features, stored_key_cache, stored_value_cache, cosine[:share],
                sine[:share], filled_lengths, query_columns, key_columns,
            )

    with jax.named_scope("to_head_rows"):
        attended = crossing_exchange(attended, "to_head_rows")
        (block,), _ = call(
            functools.partial(assemble_kernel, count),
            [array((count * share, query_columns))],
            [pltpu.VMEM((count, share, query_columns), jnp.float32)],
            [attended[k] for k in order("to_head_rows", count)],
            "assemble",
            4,
        )
    with jax.named_scope("gather_gx"):
        blocks = exchange([block] * count, "gx", "gather_gx")
        output_weights += call(
            None, [], [], [], "fetch_output", 4, loads=[load(2)], after=[block]
        )[1]
    with jax.named_scope("output"):
        products, _ = call(
            functools.partial(output_kernel, count),
            [array((count * share, out_columns))] * count,
            [pltpu.VMEM((count, count * share, query_columns), jnp.bfloat16)],
            [*(blocks[k] for k in order("gather_gx", count)), *output_weights],
            "output",
            8,
            flops=2 * count * count * share * out_rows * out_columns,
        )
    with jax.named_scope("sum_gy"):
        products = exchange(products, "gy", "sum_gy")
        (result,), _ = call(
            functools.partial(add_kernel, count),
            [array((rows, out_columns))],
            [],
            [products[k] for k in order("sum_gy", count)],
            "add",
            8,
        )
        return result


def attend_narrow(
    owned, used, features, key_rows, value_rows, cosine, sine, lengths, query_columns, key_columns
):
    count = len(owned)
    share, slots, cache_width = key_rows.shape
    kv_heads = cache_width // HEAD_SIZE
    group = query_columns * count // HEAD_SIZE // kv_heads
    me = lax.axis_index("gy")
    order = me ^ jnp.arange(count)
    stacked = jnp.stack(owned).astype(jnp.float32)
    squares = jnp.sum(stacked[0, :, -LANES:], axis=1)
    row_scale = lax.rsqrt(squares / features + EPSILON)[:, None]
    stacked = jnp.take(stacked, order, axis=0)

    def columns(first, size):
        block = stacked[:, :, first : first + size]
        return row_scale * block.transpose(1, 0, 2).reshape(share, count * size)

    def rotary(heads):
        swapped = jnp.concatenate(
            [heads[..., HEAD_SIZE // 2 :], heads[..., : HEAD_SIZE // 2]], axis=-1
        )
        shape = (share,) + (1,) * (heads.ndim - 2) + (HEAD_SIZE,)
        return (heads * cosine.reshape(shape) + swapped * sine.reshape(shape)).astype(jnp.bfloat16)

    query = rotary(columns(0, query_columns).reshape(share, kv_heads, group, HEAD_SIZE))
    fresh_key = rotary(
        columns(query_columns, key_columns).reshape(share, kv_heads, HEAD_SIZE)
    )
    fresh_value = columns(query_columns + key_columns, key_columns).astype(jnp.bfloat16)
    key_heads = key_rows.reshape(share, slots, kv_heads, HEAD_SIZE)
    value_heads = value_rows.reshape(share, slots, kv_heads, HEAD_SIZE)
    scale = 1.0 / HEAD_SIZE**0.5
    scores = scale * jnp.einsum(
        "nkgd,nlkd->nkgl", query, key_heads, preferred_element_type=jnp.float32
    )
    own = scale * jnp.einsum(
        "nkgd,nkd->nkg", query, fresh_key, preferred_element_type=jnp.float32
    )
    valid = jnp.arange(slots)[None, None, None, :] < lengths[:, None, None, None]
    scores = jnp.where(valid, scores, -1e30)
    top = jnp.maximum(jnp.max(scores, axis=-1), own)
    weights = jnp.where(valid, jnp.exp(scores - top[..., None]), 0.0)
    own_weight = jnp.exp(own - top)
    total = jnp.sum(weights, axis=-1) + own_weight
    mixed = jnp.einsum(
        "nkgl,nlkd->nkgd",
        weights.astype(jnp.bfloat16),
        value_heads,
        preferred_element_type=jnp.float32,
    )
    own_weight = own_weight.astype(jnp.bfloat16).astype(jnp.float32)
    mixed = mixed + own_weight[..., None] * fresh_value.reshape(
        share, kv_heads, 1, HEAD_SIZE
    ).astype(jnp.float32)
    mixed = (mixed / total[..., None]).astype(jnp.bfloat16)
    blocks = mixed.reshape(share, count, query_columns).transpose(1, 0, 2)
    blocks = jnp.take(blocks, order, axis=0)
    return [blocks[offset] for offset in range(count)]


def solution(mesh):
    placed = (
        P(("parts", "gy"), "gx"),
        P("gx"),
        P("gx", "gy"),
        P("gx", "gy"),
        P("gx", "gy"),
        P("gy", "gx"),
        P(("parts", "gx", "gy"), None, None),
        P(("parts", "gx", "gy"), None, None),
        P(("parts", "gx", "gy")),
    )
    return jax.shard_map(
        per_device, mesh=mesh, in_specs=placed, out_specs=P(("parts", "gy"), "gx"), check_vma=False
    )
```

```python
import functools
import math

import jax
import jax.numpy as jnp
from jax import lax
from jax.experimental import pallas as pl
from jax.experimental.pallas import tpu as pltpu
from jax.sharding import PartitionSpec as P

HEAD_SIZE = 128
LANES = 128
EPSILON = 1e-05
ORDERS = {
    "hidden": (2, 3, 1),
    "sum_gx": (2, 1, 3),
    "to_owner": (2, 3, 1),
    "to_head_rows": (2, 3, 1),
    "gather_gx": (2, 1, 3),
    "sum_gy": (2, 1, 3),
}
CUTS = (0, 3, 5, 8)
LOADS = len(CUTS) - 1
FIRST = 4
VMEM = pl.BlockSpec(memory_space=pltpu.VMEM)


def square_lanes(total):
    high = total.astype(jnp.bfloat16).astype(jnp.float32)
    rest = total - high
    middle = rest.astype(jnp.bfloat16).astype(jnp.float32)
    lane = lax.broadcasted_iota(jnp.int32, (total.shape[0], LANES), 1)
    low = rest - middle
    return jnp.where(lane == 0, high, jnp.where(lane == 1, middle, jnp.where(lane == 2, low, 0.0)))


def padded(left):
    missing = -left.shape[0] % 128
    if not missing:
        return left
    return jnp.concatenate([left, jnp.zeros((missing, left.shape[1]), left.dtype)], axis=0)


def project_kernel(count, width, *refs):
    pieces = [refs[order("hidden", count).index(offset)] for offset in range(count)]
    gain, w_query, key_weight, value_weight = refs[count : count + 4]
    outs, (held,) = refs[count + 4 : 2 * count + 4], refs[2 * count + 4 :]
    flip = lax.axis_index("gx") ^ lax.axis_index("gy") ^ 1
    gains = gain[...].astype(jnp.float32)[None, :]
    rows = pieces[0].shape[0]
    scaled = []
    for offset in range(count):
        states = pieces[offset][...].astype(jnp.float32)
        scaled.append((states * gains).astype(jnp.bfloat16))
        held[flip ^ offset, :, width - LANES :] = square_lanes(
            jnp.sum(states * states, axis=1, keepdims=True)
        ).astype(jnp.bfloat16)
    left = padded(jnp.concatenate(scaled, axis=0))
    start = 0
    for weight in (w_query, key_weight, value_weight):
        columns = weight.shape[1]
        step = min(columns, 512)
        for first in range(0, columns, step):
            product = jnp.dot(
                left, weight[:, first : first + step], preferred_element_type=jnp.float32
            ).astype(jnp.bfloat16)
            for offset in range(count):
                held[flip ^ offset, :, start : start + step] = product[
                    offset * rows : (offset + 1) * rows
                ]
            start += step
    for offset in range(count):
        outs[offset][...] = held[offset]
        if start < width - LANES:
            outs[offset][:, start : width - LANES] = jnp.zeros(
                (rows, width - LANES - start), jnp.bfloat16
            )


def combine_kernel(count, *refs):
    pieces = [refs[order("sum_gx", count).index(offset)] for offset in range(count)]
    outs, (held,) = refs[count : 2 * count], refs[2 * count :]
    total = pieces[0][...].astype(jnp.float32)
    for piece in pieces[1:]:
        total = total + piece[...].astype(jnp.float32)
    share = held.shape[1]
    width = total.shape[1]
    squares = square_lanes(jnp.sum(total[:, width - LANES :], axis=1, keepdims=True))
    for owner in range(count):
        rows = slice(owner * share, (owner + 1) * share)
        held[owner, :, : width - LANES] = total[rows, : width - LANES]
        held[owner, :, width - LANES :] = squares[rows]
    me = lax.axis_index("gy")
    for offset in range(count):
        outs[offset][...] = held[me ^ offset].astype(jnp.bfloat16)


def spread(rows, group):
    repeat = min(group, max(1, 8 // rows.shape[0]))
    tile = jnp.concatenate([rows] * repeat, axis=0) if repeat > 1 else rows
    wide = jnp.broadcast_to(tile[None], (group // repeat, *tile.shape))
    return wide.reshape(group * rows.shape[0], rows.shape[1])


def attend_kernel(count, group, features, *refs):
    pieces = [refs[order("to_owner", count).index(offset)] for offset in range(count)]
    keys, values, cosines, sines, filled = refs[count : count + 5]
    outs = refs[count + 5 :]
    share, slots = keys.shape[0], keys.shape[1]
    rows = share * group
    scale = 1.0 / HEAD_SIZE**0.5
    width = pieces[0].shape[1]
    me = lax.axis_index("gy")
    cosine, sine = cosines[...], sines[...]
    squares = jnp.sum(
        pieces[0][:, width - LANES :].astype(jnp.float32), axis=1, keepdims=True
    )
    row_scale = lax.rsqrt(squares / features + EPSILON)
    row_scales = spread(row_scale, group)
    item = lax.broadcasted_iota(jnp.int32, (rows, 1), 0) % share
    valid = lax.broadcasted_iota(jnp.int32, (rows, slots), 1) < filled[:, :1]
    states, scores = [], []
    for offset in range(count):
        piece = pieces[offset][...].astype(jnp.float32)
        head = me ^ offset
        lanes = pl.ds(pl.multiple_of(head * HEAD_SIZE, HEAD_SIZE), HEAD_SIZE)
        query = jnp.concatenate(
            [piece[:, h * HEAD_SIZE : (h + 1) * HEAD_SIZE] for h in range(group)], axis=0
        )
        query = query * row_scales
        query = query * cosine + pltpu.roll(query, HEAD_SIZE // 2, 1) * sine
        query = query.astype(jnp.bfloat16)
        first = group * HEAD_SIZE
        fresh_key = spread(piece[:, first : first + HEAD_SIZE], group) * row_scales
        fresh_key = fresh_key * cosine + pltpu.roll(fresh_key, HEAD_SIZE // 2, 1) * sine
        fresh_key = fresh_key.astype(jnp.bfloat16).astype(jnp.float32)
        first = first + HEAD_SIZE
        fresh_value = spread(piece[:, first : first + HEAD_SIZE], group) * row_scales
        fresh_value = fresh_value.astype(jnp.bfloat16).astype(jnp.float32)
        own = jnp.sum(query.astype(jnp.float32) * fresh_key, axis=1, keepdims=True) * scale
        states.append((lanes, own, fresh_value))
        products = [
            lax.dot_general(
                query,
                keys[n, :, lanes],
                (((1,), (1,)), ((), ())),
                preferred_element_type=jnp.float32,
            )
            for n in range(share)
        ]
        score = products[0]
        for n in range(1, share):
            score = jnp.where(item == n, products[n], score)
        scores.append(jnp.where(valid, score * scale, -1e30))
    tops = [
        jnp.maximum(jnp.max(score, axis=1, keepdims=True), own)
        for score, (_, own, _) in zip(scores, states)
    ]
    weights = [
        jnp.where(valid, jnp.exp(score - top), 0.0) for score, top in zip(scores, tops)
    ]
    for offset, (lanes, own, fresh_value) in enumerate(states):
        own_weight = jnp.exp(own - tops[offset])
        total = jnp.sum(weights[offset], axis=1, keepdims=True) + own_weight
        mixed = own_weight.astype(jnp.bfloat16).astype(jnp.float32) * fresh_value
        for n in range(share):
            mixed = mixed + jnp.dot(
                jnp.where(item == n, weights[offset], 0.0).astype(jnp.bfloat16),
                values[n, :, lanes],
                preferred_element_type=jnp.float32,
            )
        mixed = mixed / total
        outs[offset][...] = jnp.concatenate(
            [mixed[h * share : (h + 1) * share] for h in range(group)], axis=1
        ).astype(jnp.bfloat16)


def assemble_kernel(count, *refs):
    pieces = [refs[order("to_head_rows", count).index(offset)] for offset in range(count)]
    out, held = refs[count], refs[count + 1]
    me = lax.axis_index("gy")
    for offset in range(count):
        held[me ^ offset] = pieces[offset][...].astype(jnp.float32)
    out[...] = jnp.concatenate([held[n] for n in range(count)], axis=0).astype(jnp.bfloat16)


def output_kernel(count, begin, earlier, *refs):
    pieces = [refs[order("gather_gx", count).index(offset)] for offset in range(count)]
    weights = refs[count : count + LOADS]
    before = refs[count + LOADS : count + LOADS + earlier]
    refs = refs[count + LOADS + earlier :]
    outs, (held,) = refs[:count], refs[count:]
    flip = lax.axis_index("gx") ^ lax.axis_index("gy") ^ 1
    for offset in range(count):
        held[flip ^ offset] = pieces[offset][...]
    if earlier:
        outs[1][:, :begin] = before[0][...]
    rows = held.shape[1]
    left = padded(held[...].reshape(count * rows, held.shape[2]))
    columns = outs[0].shape[1]
    step = min(columns, 512)
    for first in range(0, columns, step):
        product, start = 0.0, 0
        for weight in weights:
            depth = weight.shape[0]
            product = product + jnp.dot(
                left[:, start : start + depth],
                weight[:, begin + first : begin + first + step],
                preferred_element_type=jnp.float32,
            )
            start += depth
        product = product.astype(jnp.bfloat16)
        for offset in range(count):
            shift = begin if earlier and offset == 1 else 0
            outs[offset][:, shift + first : shift + first + step] = product[
                offset * rows : (offset + 1) * rows
            ]


def relay_kernel(mine, relayed, out):
    out[...] = (mine[...].astype(jnp.float32) + relayed[...].astype(jnp.float32)).astype(
        jnp.bfloat16
    )


def add_kernel(terms, *refs):
    whole, out = refs[-2], refs[-1]
    start = 0
    for first in range(0, len(refs) - 2, terms):
        end = start + refs[first].shape[1]
        total = whole[:, start:end].astype(jnp.float32)
        for piece in refs[first : first + terms]:
            total = total + piece[...].astype(jnp.float32)
        out[:, start:end] = total.astype(jnp.bfloat16)
        start = end


def rotary_kernel(share, lengths, cosines, sines, filled):
    rows = cosines.shape[0]
    item = lax.broadcasted_iota(jnp.int32, (rows, HEAD_SIZE), 0) % share
    column = lax.broadcasted_iota(jnp.int32, (rows, HEAD_SIZE), 1)
    half = HEAD_SIZE // 2
    length = jnp.zeros((rows, HEAD_SIZE), jnp.int32)
    for n in range(share):
        length = jnp.where(item == n, lengths[n], length)
    power = (column % half).astype(jnp.float32) * (2.0 / HEAD_SIZE)
    angles = length.astype(jnp.float32) * jnp.exp(-math.log(500000.0) * power)
    sine = jnp.sin(angles)
    cosines[...] = jnp.cos(angles)
    sines[...] = jnp.where(column < half, -sine, sine)
    filled[...] = length


def loading(kernel, loads, counts, *refs):
    skip, inputs, outputs = counts
    many = len(loads)
    sources, refs = refs[:many], refs[many + skip :]
    if many:
        targets, sems = refs[inputs + outputs : inputs + outputs + many], refs[-1]
        refs = refs[: inputs + outputs] + refs[inputs + outputs + many : -1]
    copies = [
        pltpu.make_async_copy(sources[n].at[pl.ds(first, rows)], targets[n], sems.at[n])
        for n, (first, rows) in enumerate(loads)
    ]
    for copy in copies:
        copy.start()
    if kernel is not None and copies:
        pl.when(lax.axis_index("gy") >= 0)(lambda: kernel(*refs))
    elif kernel is not None:
        kernel(*refs)
    for copy in copies:
        copy.wait()


def call(kernel, outs, scratch, args, name, limit, scalars=0, loads=(), flops=0, after=()):
    arrays = [pltpu.with_memory_space_constraint(load[0], pltpu.HBM) for load in loads]
    parts = [load[1:] for load in loads]
    size = sum(4 * rows * array.shape[1] for array, _, rows in loads)
    size += sum(a.size * a.dtype.itemsize for a in (*args, *outs))
    results = pl.pallas_call(
        functools.partial(loading, kernel, parts, (len(after), len(args), len(outs))),
        out_shape=[*outs, *(pltpu.VMEM((rows, a.shape[1]), a.dtype) for a, _, rows in loads)],
        in_specs=[pl.BlockSpec(memory_space=pltpu.HBM)] * len(loads)
        + [pl.BlockSpec(memory_space=pl.ANY)] * len(after)
        + [VMEM] * (len(args) - scalars)
        + [pl.BlockSpec(memory_space=pltpu.SMEM)] * scalars,
        out_specs=[VMEM] * (len(outs) + len(loads)),
        scratch_shapes=scratch
        + ([pltpu.SemaphoreType.DMA((len(loads),))] if loads else []),
        cost_estimate=pl.CostEstimate(
            flops=flops, bytes_accessed=size, transcendentals=0
        ),
        compiler_params=pltpu.CompilerParams(vmem_limit_bytes=limit << 20),
        name=name,
    )(*arrays, *after, *args)
    return results[: len(outs)], results[len(outs) :]


def array(shape, dtype=jnp.bfloat16):
    return jax.ShapeDtypeStruct(shape, dtype)


def order(name, count):
    if count == len(ORDERS[name]) + 1:
        return (0, *ORDERS[name])
    return (0, *range(count - 1, 0, -1))


def exchange(pieces, axis, name):
    count = len(pieces)
    result = list(pieces)
    for offset in order(name, count)[1:]:
        result[offset] = lax.ppermute(
            pieces[offset], axis, [(n, n ^ offset) for n in range(count)]
        )
    return result


def crossing_exchange(pieces, name):
    count = len(pieces)
    result = list(pieces)
    for offset in (*order(name, count)[1:], 0):
        result[offset] = lax.ppermute(
            pieces[offset],
            ("gx", "gy"),
            [(n, (n ^ count) ^ offset) for n in range(lax.axis_size("gx") * count)],
        )
    return result


def per_device(
    hidden_states,
    norm_gain,
    w_query,
    key_weight,
    value_weight,
    w_output,
    stored_key_cache,
    stored_value_cache,
    filled_lengths,
):
    across, down = lax.axis_size("gx"), lax.axis_size("gy")
    assert across == down and across & (across - 1) == 0
    count = down
    share, slots, cache_width = stored_key_cache.shape
    rows, depth = hidden_states.shape
    features = depth * across
    query_columns, key_columns = w_query.shape[1], key_weight.shape[1]
    kv_heads = cache_width // HEAD_SIZE
    group = query_columns * down // HEAD_SIZE // kv_heads

    used = query_columns + 2 * key_columns
    width = -(-used // LANES) * LANES + LANES
    out_rows, out_columns = w_output.shape
    cuts = [out_rows * cut // 8 for cut in CUTS]

    def load(index):
        return w_output, cuts[index], cuts[index + 1] - cuts[index]

    with jax.named_scope("gather_hidden"):
        gathered = exchange([hidden_states] * count, "gy", "hidden")
    with jax.named_scope("fetch_query"):
        _, weights = call(None, [], [], [], "fetch_query", 4, loads=[(w_query, 0, depth)])
    with jax.named_scope("project"):
        partial, output_weights = call(
            functools.partial(project_kernel, count, width),
            [array((rows, width))] * count,
            [pltpu.VMEM((count, rows, width), jnp.bfloat16)],
            [
                *(gathered[k] for k in order("hidden", count)),
                norm_gain,
                *weights,
                key_weight,
                value_weight,
            ],
            "project",
            8,
            loads=[load(0)],
            flops=2 * count * rows * depth * used,
        )
    with jax.named_scope("sum_gx"):
        received = exchange(partial, "gx", "sum_gx")
        table = array((share * group, HEAD_SIZE), jnp.float32)
        (cosine, sine, filled), loaded = call(
            functools.partial(rotary_kernel, share),
            [table, table, array(table.shape, jnp.int32)],
            [],
            [filled_lengths],
            "fetch_output",
            4,
            scalars=1,
            loads=[load(1)],
            after=partial[:1],
        )
        output_weights += loaded
        owned, _ = call(
            functools.partial(combine_kernel, count),
            [array((share, width))] * count,
            [pltpu.VMEM((count, share, width), jnp.float32)],
            [received[k] for k in order("sum_gx", count)],
            "combine",
            4,
            after=output_weights[1:],
        )
    with jax.named_scope("to_owner"):
        owned = crossing_exchange(owned, "to_owner")

    with jax.named_scope("attend"):
        if key_columns == HEAD_SIZE:
            attended, _ = call(
                functools.partial(attend_kernel, count, group, features),
                [array((share, query_columns))] * count,
                [],
                [
                    *(owned[k] for k in order("to_owner", count)),
                    stored_key_cache,
                    stored_value_cache,
                    cosine,
                    sine,
                    filled,
                ],
                "attend",
                8,
            )
        else:
            attended = attend_narrow(
                owned, used, features, stored_key_cache, stored_value_cache, cosine[:share],
                sine[:share], filled_lengths, query_columns, key_columns,
            )

    with jax.named_scope("to_head_rows"):
        attended = crossing_exchange(attended, "to_head_rows")
        (block,), _ = call(
            functools.partial(assemble_kernel, count),
            [array((count * share, query_columns))],
            [pltpu.VMEM((count, share, query_columns), jnp.float32)],
            [attended[k] for k in order("to_head_rows", count)],
            "assemble",
            4,
        )
    with jax.named_scope("gather_gx"):
        blocks = exchange([block] * count, "gx", "gather_gx")
        output_weights += call(
            None, [], [], [], "fetch_output", 4, loads=[load(2)], after=[block]
        )[1]
    cut = out_columns * FIRST // 8
    pair = [(n, n ^ 1) for n in range(count)]
    terms, before = [], []
    for begin, end in ((0, cut), (cut, out_columns)):
        shapes = [(count * share, end - begin)] * count
        if begin:
            shapes[1] = (count * share, end)
        with jax.named_scope("output"):
            parts, _ = call(
                functools.partial(output_kernel, count, begin, len(before)),
                [array(shape) for shape in shapes],
                [pltpu.VMEM((count, count * share, query_columns), jnp.bfloat16)],
                [
                    *(blocks[k] for k in order("gather_gx", count)),
                    *output_weights,
                    *before,
                ],
                "output",
                8,
                flops=2 * count * count * share * out_rows * (end - begin),
            )
        before = [parts[1]]
        terms.append(parts[0])
        with jax.named_scope("sum_gy"):
            for offset in range(2, count, 2):
                relayed = lax.ppermute(parts[offset + 1], "gy", pair)
                (both,), _ = call(
                    relay_kernel,
                    [array(shapes[offset])],
                    [],
                    [parts[offset], relayed],
                    "relay",
                    4,
                )
                terms.append(
                    lax.ppermute(both, "gy", [(n, n ^ offset) for n in range(count)])
                )
    with jax.named_scope("sum_gy"):
        (result,), _ = call(
            functools.partial(add_kernel, len(terms) // 2),
            [array((rows, out_columns))],
            [],
            [*terms, lax.ppermute(before[0], "gy", pair)],
            "add",
            8,
        )
        return result


def attend_narrow(
    owned, used, features, key_rows, value_rows, cosine, sine, lengths, query_columns, key_columns
):
    count = len(owned)
    share, slots, cache_width = key_rows.shape
    kv_heads = cache_width // HEAD_SIZE
    group = query_columns * count // HEAD_SIZE // kv_heads
    me = lax.axis_index("gy")
    order = me ^ jnp.arange(count)
    stacked = jnp.stack(owned).astype(jnp.float32)
    squares = jnp.sum(stacked[0, :, -LANES:], axis=1)
    row_scale = lax.rsqrt(squares / features + EPSILON)[:, None]
    stacked = jnp.take(stacked, order, axis=0)

    def columns(first, size):
        block = stacked[:, :, first : first + size]
        return row_scale * block.transpose(1, 0, 2).reshape(share, count * size)

    def rotary(heads):
        swapped = jnp.concatenate(
            [heads[..., HEAD_SIZE // 2 :], heads[..., : HEAD_SIZE // 2]], axis=-1
        )
        shape = (share,) + (1,) * (heads.ndim - 2) + (HEAD_SIZE,)
        return (heads * cosine.reshape(shape) + swapped * sine.reshape(shape)).astype(jnp.bfloat16)

    query = rotary(columns(0, query_columns).reshape(share, kv_heads, group, HEAD_SIZE))
    fresh_key = rotary(
        columns(query_columns, key_columns).reshape(share, kv_heads, HEAD_SIZE)
    )
    fresh_value = columns(query_columns + key_columns, key_columns).astype(jnp.bfloat16)
    key_heads = key_rows.reshape(share, slots, kv_heads, HEAD_SIZE)
    value_heads = value_rows.reshape(share, slots, kv_heads, HEAD_SIZE)
    scale = 1.0 / HEAD_SIZE**0.5
    scores = scale * jnp.einsum(
        "nkgd,nlkd->nkgl", query, key_heads, preferred_element_type=jnp.float32
    )
    own = scale * jnp.einsum(
        "nkgd,nkd->nkg", query, fresh_key, preferred_element_type=jnp.float32
    )
    valid = jnp.arange(slots)[None, None, None, :] < lengths[:, None, None, None]
    scores = jnp.where(valid, scores, -1e30)
    top = jnp.maximum(jnp.max(scores, axis=-1), own)
    weights = jnp.where(valid, jnp.exp(scores - top[..., None]), 0.0)
    own_weight = jnp.exp(own - top)
    total = jnp.sum(weights, axis=-1) + own_weight
    mixed = jnp.einsum(
        "nkgl,nlkd->nkgd",
        weights.astype(jnp.bfloat16),
        value_heads,
        preferred_element_type=jnp.float32,
    )
    own_weight = own_weight.astype(jnp.bfloat16).astype(jnp.float32)
    mixed = mixed + own_weight[..., None] * fresh_value.reshape(
        share, kv_heads, 1, HEAD_SIZE
    ).astype(jnp.float32)
    mixed = (mixed / total[..., None]).astype(jnp.bfloat16)
    blocks = mixed.reshape(share, count, query_columns).transpose(1, 0, 2)
    blocks = jnp.take(blocks, order, axis=0)
    return [blocks[offset] for offset in range(count)]


def solution(mesh):
    placed = (
        P(("parts", "gy"), "gx"),
        P("gx"),
        P("gx", "gy"),
        P("gx", "gy"),
        P("gx", "gy"),
        P("gy", "gx"),
        P(("parts", "gx", "gy"), None, None),
        P(("parts", "gx", "gy"), None, None),
        P(("parts", "gx", "gy")),
    )
    return jax.shard_map(
        per_device, mesh=mesh, in_specs=placed, out_specs=P(("parts", "gy"), "gx"), check_vma=False
    )
```

```python
import functools
import math

import jax
import jax.numpy as jnp
from jax import lax
from jax.experimental import pallas as pl
from jax.experimental.pallas import tpu as pltpu
from jax.sharding import PartitionSpec as P

HEAD_SIZE = 128
LANES = 128
EPSILON = 1e-05
ORDERS = {
    "hidden": (2, 3, 1),
    "sum_gx": (2, 1, 3),
    "to_owner": (2, 3, 1),
    "to_head_rows": (2, 3, 1),
    "gather_gx": (2, 1, 3),
    "sum_gy": (2, 1, 3),
}
CUTS = (0, 3, 5, 8)
LOADS = len(CUTS) - 1
VMEM = pl.BlockSpec(memory_space=pltpu.VMEM)


def square_lanes(total):
    high = total.astype(jnp.bfloat16).astype(jnp.float32)
    rest = total - high
    middle = rest.astype(jnp.bfloat16).astype(jnp.float32)
    lane = lax.broadcasted_iota(jnp.int32, (total.shape[0], LANES), 1)
    low = rest - middle
    return jnp.where(lane == 0, high, jnp.where(lane == 1, middle, jnp.where(lane == 2, low, 0.0)))


def padded(left):
    missing = -left.shape[0] % 128
    if not missing:
        return left
    return jnp.concatenate([left, jnp.zeros((missing, left.shape[1]), left.dtype)], axis=0)


def project_kernel(count, width, *refs):
    pieces = [refs[order("hidden", count).index(offset)] for offset in range(count)]
    gain, w_query, key_weight, value_weight = refs[count : count + 4]
    outs, (held,) = refs[count + 4 : 2 * count + 4], refs[2 * count + 4 :]
    flip = lax.axis_index("gx") ^ lax.axis_index("gy") ^ 1
    gains = gain[...].astype(jnp.float32)[None, :]
    rows = pieces[0].shape[0]
    scaled = []
    for offset in range(count):
        states = pieces[offset][...].astype(jnp.float32)
        scaled.append((states * gains).astype(jnp.bfloat16))
        held[flip ^ offset, :, width - LANES :] = square_lanes(
            jnp.sum(states * states, axis=1, keepdims=True)
        ).astype(jnp.bfloat16)
    left = padded(jnp.concatenate(scaled, axis=0))
    start = 0
    for weight in (w_query, key_weight, value_weight):
        columns = weight.shape[1]
        step = min(columns, 512)
        for first in range(0, columns, step):
            product = jnp.dot(
                left, weight[:, first : first + step], preferred_element_type=jnp.float32
            ).astype(jnp.bfloat16)
            for offset in range(count):
                held[flip ^ offset, :, start : start + step] = product[
                    offset * rows : (offset + 1) * rows
                ]
            start += step
    for offset in range(count):
        outs[offset][...] = held[offset]
        if start < width - LANES:
            outs[offset][:, start : width - LANES] = jnp.zeros(
                (rows, width - LANES - start), jnp.bfloat16
            )


def combine_kernel(count, *refs):
    pieces = [refs[order("sum_gx", count).index(offset)] for offset in range(count)]
    outs, (held,) = refs[count : 2 * count], refs[2 * count :]
    total = pieces[0][...].astype(jnp.float32)
    for piece in pieces[1:]:
        total = total + piece[...].astype(jnp.float32)
    share = held.shape[1]
    width = total.shape[1]
    squares = square_lanes(jnp.sum(total[:, width - LANES :], axis=1, keepdims=True))
    for owner in range(count):
        rows = slice(owner * share, (owner + 1) * share)
        held[owner, :, : width - LANES] = total[rows, : width - LANES]
        held[owner, :, width - LANES :] = squares[rows]
    me = lax.axis_index("gy")
    for offset in range(count):
        outs[offset][...] = held[me ^ offset].astype(jnp.bfloat16)


def spread(rows, group):
    repeat = min(group, max(1, 8 // rows.shape[0]))
    tile = jnp.concatenate([rows] * repeat, axis=0) if repeat > 1 else rows
    wide = jnp.broadcast_to(tile[None], (group // repeat, *tile.shape))
    return wide.reshape(group * rows.shape[0], rows.shape[1])


def attend_kernel(offsets, group, features, *refs):
    count = len(offsets)
    pieces = refs[:count]
    keys, values, cosines, sines, filled = refs[count : count + 5]
    outs = refs[count + 5 :]
    share, slots = keys.shape[0], keys.shape[1]
    rows = share * group
    scale = 1.0 / HEAD_SIZE**0.5
    width = pieces[0].shape[1]
    me = lax.axis_index("gy")
    cosine, sine = cosines[...], sines[...]
    squares = jnp.sum(
        pieces[0][:, width - LANES :].astype(jnp.float32), axis=1, keepdims=True
    )
    row_scale = lax.rsqrt(squares / features + EPSILON)
    row_scales = spread(row_scale, group)
    item = lax.broadcasted_iota(jnp.int32, (rows, 1), 0) % share
    valid = lax.broadcasted_iota(jnp.int32, (rows, slots), 1) < filled[:, :1]
    states, scores = [], []
    for piece, offset in zip(pieces, offsets):
        piece = piece[...].astype(jnp.float32)
        head = me ^ offset
        lanes = pl.ds(pl.multiple_of(head * HEAD_SIZE, HEAD_SIZE), HEAD_SIZE)
        query = jnp.concatenate(
            [piece[:, h * HEAD_SIZE : (h + 1) * HEAD_SIZE] for h in range(group)], axis=0
        )
        query = query * row_scales
        query = query * cosine + pltpu.roll(query, HEAD_SIZE // 2, 1) * sine
        query = query.astype(jnp.bfloat16)
        first = group * HEAD_SIZE
        fresh_key = spread(piece[:, first : first + HEAD_SIZE], group) * row_scales
        fresh_key = fresh_key * cosine + pltpu.roll(fresh_key, HEAD_SIZE // 2, 1) * sine
        fresh_key = fresh_key.astype(jnp.bfloat16).astype(jnp.float32)
        first = first + HEAD_SIZE
        fresh_value = spread(piece[:, first : first + HEAD_SIZE], group) * row_scales
        fresh_value = fresh_value.astype(jnp.bfloat16).astype(jnp.float32)
        own = jnp.sum(query.astype(jnp.float32) * fresh_key, axis=1, keepdims=True) * scale
        states.append((lanes, own, fresh_value))
        products = [
            lax.dot_general(
                query,
                keys[n, :, lanes],
                (((1,), (1,)), ((), ())),
                preferred_element_type=jnp.float32,
            )
            for n in range(share)
        ]
        score = products[0]
        for n in range(1, share):
            score = jnp.where(item == n, products[n], score)
        scores.append(jnp.where(valid, score * scale, -1e30))
    tops = [
        jnp.maximum(jnp.max(score, axis=1, keepdims=True), own)
        for score, (_, own, _) in zip(scores, states)
    ]
    weights = [
        jnp.where(valid, jnp.exp(score - top), 0.0) for score, top in zip(scores, tops)
    ]
    for offset, (lanes, own, fresh_value) in enumerate(states):
        own_weight = jnp.exp(own - tops[offset])
        total = jnp.sum(weights[offset], axis=1, keepdims=True) + own_weight
        mixed = own_weight.astype(jnp.bfloat16).astype(jnp.float32) * fresh_value
        for n in range(share):
            mixed = mixed + jnp.dot(
                jnp.where(item == n, weights[offset], 0.0).astype(jnp.bfloat16),
                values[n, :, lanes],
                preferred_element_type=jnp.float32,
            )
        mixed = mixed / total
        outs[offset][...] = jnp.concatenate(
            [mixed[h * share : (h + 1) * share] for h in range(group)], axis=1
        ).astype(jnp.bfloat16)


def assemble_kernel(count, *refs):
    pieces = [refs[order("to_head_rows", count).index(offset)] for offset in range(count)]
    out, held = refs[count], refs[count + 1]
    me = lax.axis_index("gy")
    for offset in range(count):
        held[me ^ offset] = pieces[offset][...].astype(jnp.float32)
    out[...] = jnp.concatenate([held[n] for n in range(count)], axis=0).astype(jnp.bfloat16)


def output_kernel(count, *refs):
    pieces = [refs[order("gather_gx", count).index(offset)] for offset in range(count)]
    weights = refs[count : count + LOADS]
    outs, (held,) = refs[count + LOADS : 2 * count + LOADS], refs[2 * count + LOADS :]
    flip = lax.axis_index("gx") ^ lax.axis_index("gy") ^ 1
    for offset in range(count):
        held[flip ^ offset] = pieces[offset][...]
    rows = held.shape[1]
    left = padded(held[...].reshape(count * rows, held.shape[2]))
    columns = weights[0].shape[1]
    step = min(columns, 512)
    for first in range(0, columns, step):
        product, start = 0.0, 0
        for weight in weights:
            depth = weight.shape[0]
            product = product + jnp.dot(
                left[:, start : start + depth],
                weight[:, first : first + step],
                preferred_element_type=jnp.float32,
            )
            start += depth
        product = product.astype(jnp.bfloat16)
        for offset in range(count):
            outs[offset][:, first : first + step] = product[offset * rows : (offset + 1) * rows]


def add_kernel(count, *refs):
    total = refs[0][...].astype(jnp.float32)
    for piece in refs[1:count]:
        total = total + piece[...].astype(jnp.float32)
    refs[count][...] = total.astype(jnp.bfloat16)


def rotary_kernel(share, lengths, cosines, sines, filled):
    rows = cosines.shape[0]
    item = lax.broadcasted_iota(jnp.int32, (rows, HEAD_SIZE), 0) % share
    column = lax.broadcasted_iota(jnp.int32, (rows, HEAD_SIZE), 1)
    half = HEAD_SIZE // 2
    length = jnp.zeros((rows, HEAD_SIZE), jnp.int32)
    for n in range(share):
        length = jnp.where(item == n, lengths[n], length)
    power = (column % half).astype(jnp.float32) * (2.0 / HEAD_SIZE)
    angles = length.astype(jnp.float32) * jnp.exp(-math.log(500000.0) * power)
    sine = jnp.sin(angles)
    cosines[...] = jnp.cos(angles)
    sines[...] = jnp.where(column < half, -sine, sine)
    filled[...] = length


def loading(kernel, loads, counts, *refs):
    skip, inputs, outputs = counts
    many = len(loads)
    sources, refs = refs[:many], refs[many + skip :]
    if many:
        targets, sems = refs[inputs + outputs : inputs + outputs + many], refs[-1]
        refs = refs[: inputs + outputs] + refs[inputs + outputs + many : -1]
    copies = [
        pltpu.make_async_copy(sources[n].at[pl.ds(first, rows)], targets[n], sems.at[n])
        for n, (first, rows) in enumerate(loads)
    ]
    for copy in copies:
        copy.start()
    if kernel is not None and copies:
        pl.when(lax.axis_index("gy") >= 0)(lambda: kernel(*refs))
    elif kernel is not None:
        kernel(*refs)
    for copy in copies:
        copy.wait()


def call(kernel, outs, scratch, args, name, limit, scalars=0, loads=(), flops=0, after=()):
    arrays = [pltpu.with_memory_space_constraint(load[0], pltpu.HBM) for load in loads]
    parts = [load[1:] for load in loads]
    size = sum(2 * rows * array.shape[1] for array, _, rows in loads)
    results = pl.pallas_call(
        functools.partial(loading, kernel, parts, (len(after), len(args), len(outs))),
        out_shape=[*outs, *(pltpu.VMEM((rows, a.shape[1]), a.dtype) for a, _, rows in loads)],
        in_specs=[pl.BlockSpec(memory_space=pltpu.HBM)] * len(loads)
        + [pl.BlockSpec(memory_space=pl.ANY)] * len(after)
        + [VMEM] * (len(args) - scalars)
        + [pl.BlockSpec(memory_space=pltpu.SMEM)] * scalars,
        out_specs=[VMEM] * (len(outs) + len(loads)),
        scratch_shapes=scratch
        + ([pltpu.SemaphoreType.DMA((len(loads),))] if loads else []),
        cost_estimate=pl.CostEstimate(
            flops=flops, bytes_accessed=2 * size + (1 << 16), transcendentals=0
        ),
        compiler_params=pltpu.CompilerParams(vmem_limit_bytes=limit << 20),
        name=name,
    )(*arrays, *after, *args)
    return results[: len(outs)], results[len(outs) :]


def array(shape, dtype=jnp.bfloat16):
    return jax.ShapeDtypeStruct(shape, dtype)


def order(name, count):
    if count == len(ORDERS[name]) + 1:
        return (0, *ORDERS[name])
    return (0, *range(count - 1, 0, -1))


def exchange(pieces, axis, name):
    count = len(pieces)
    result = list(pieces)
    for offset in order(name, count)[1:]:
        result[offset] = lax.ppermute(
            pieces[offset], axis, [(n, n ^ offset) for n in range(count)]
        )
    return result


def crossing_exchange(pieces, name):
    count = len(pieces)
    result = list(pieces)
    for offset in (*order(name, count)[1:], 0):
        result[offset] = lax.ppermute(
            pieces[offset],
            ("gx", "gy"),
            [(n, (n ^ count) ^ offset) for n in range(lax.axis_size("gx") * count)],
        )
    return result


def per_device(
    hidden_states,
    norm_gain,
    w_query,
    key_weight,
    value_weight,
    w_output,
    stored_key_cache,
    stored_value_cache,
    filled_lengths,
):
    across, down = lax.axis_size("gx"), lax.axis_size("gy")
    assert across == down and across & (across - 1) == 0
    count = down
    share, slots, cache_width = stored_key_cache.shape
    rows, depth = hidden_states.shape
    features = depth * across
    query_columns, key_columns = w_query.shape[1], key_weight.shape[1]
    kv_heads = cache_width // HEAD_SIZE
    group = query_columns * down // HEAD_SIZE // kv_heads

    used = query_columns + 2 * key_columns
    width = -(-used // LANES) * LANES + LANES
    out_rows, out_columns = w_output.shape
    cuts = [out_rows * cut // 8 for cut in CUTS]

    def load(index):
        return w_output, cuts[index], cuts[index + 1] - cuts[index]

    with jax.named_scope("gather_hidden"):
        gathered = exchange([hidden_states] * count, "gy", "hidden")
    with jax.named_scope("fetch_query"):
        _, weights = call(None, [], [], [], "fetch_query", 4, loads=[(w_query, 0, depth)])
    with jax.named_scope("project"):
        partial, output_weights = call(
            functools.partial(project_kernel, count, width),
            [array((rows, width))] * count,
            [pltpu.VMEM((count, rows, width), jnp.bfloat16)],
            [
                *(gathered[k] for k in order("hidden", count)),
                norm_gain,
                *weights,
                key_weight,
                value_weight,
            ],
            "project",
            8,
            loads=[load(0)],
            flops=2 * count * rows * depth * used,
        )
    with jax.named_scope("sum_gx"):
        received = exchange(partial, "gx", "sum_gx")
        table = array((share * group, HEAD_SIZE), jnp.float32)
        (cosine, sine, filled), loaded = call(
            functools.partial(rotary_kernel, share),
            [table, table, array(table.shape, jnp.int32)],
            [],
            [filled_lengths],
            "fetch_output",
            4,
            scalars=1,
            loads=[load(1)],
            after=partial[:1],
        )
        output_weights += loaded
        owned, _ = call(
            functools.partial(combine_kernel, count),
            [array((share, width))] * count,
            [pltpu.VMEM((count, share, width), jnp.float32)],
            [received[k] for k in order("sum_gx", count)],
            "combine",
            4,
            after=output_weights[1:],
        )
    with jax.named_scope("to_owner"):
        owned = crossing_exchange(owned, "to_owner")

    with jax.named_scope("attend"):
        if key_columns == HEAD_SIZE:
            attended = [None] * count
            taken = order("to_owner", count)
            early = len(taken) // 2
            for offsets in (taken[:early], taken[early:]):
                results, _ = call(
                    functools.partial(attend_kernel, offsets, group, features),
                    [array((share, query_columns))] * len(offsets),
                    [],
                    [
                        *(owned[k] for k in offsets),
                        stored_key_cache,
                        stored_value_cache,
                        cosine,
                        sine,
                        filled,
                    ],
                    "attend",
                    8,
                )
                for offset, result in zip(offsets, results):
                    attended[offset] = result
        else:
            attended = attend_narrow(
                owned, used, features, stored_key_cache, stored_value_cache, cosine[:share],
                sine[:share], filled_lengths, query_columns, key_columns,
            )

    with jax.named_scope("to_head_rows"):
        attended = crossing_exchange(attended, "to_head_rows")
        (block,), _ = call(
            functools.partial(assemble_kernel, count),
            [array((count * share, query_columns))],
            [pltpu.VMEM((count, share, query_columns), jnp.float32)],
            [attended[k] for k in order("to_head_rows", count)],
            "assemble",
            4,
        )
    with jax.named_scope("gather_gx"):
        blocks = exchange([block] * count, "gx", "gather_gx")
        output_weights += call(
            None, [], [], [], "fetch_output", 4, loads=[load(2)], after=[block]
        )[1]
    with jax.named_scope("output"):
        products, _ = call(
            functools.partial(output_kernel, count),
            [array((count * share, out_columns))] * count,
            [pltpu.VMEM((count, count * share, query_columns), jnp.bfloat16)],
            [*(blocks[k] for k in order("gather_gx", count)), *output_weights],
            "output",
            8,
            flops=2 * count * count * share * out_rows * out_columns,
        )
    with jax.named_scope("sum_gy"):
        products = exchange(products, "gy", "sum_gy")
        (result,), _ = call(
            functools.partial(add_kernel, count),
            [array((rows, out_columns))],
            [],
            [products[k] for k in order("sum_gy", count)],
            "add",
            8,
        )
        return result


def attend_narrow(
    owned, used, features, key_rows, value_rows, cosine, sine, lengths, query_columns, key_columns
):
    count = len(owned)
    share, slots, cache_width = key_rows.shape
    kv_heads = cache_width // HEAD_SIZE
    group = query_columns * count // HEAD_SIZE // kv_heads
    me = lax.axis_index("gy")
    order = me ^ jnp.arange(count)
    stacked = jnp.stack(owned).astype(jnp.float32)
    squares = jnp.sum(stacked[0, :, -LANES:], axis=1)
    row_scale = lax.rsqrt(squares / features + EPSILON)[:, None]
    stacked = jnp.take(stacked, order, axis=0)

    def columns(first, size):
        block = stacked[:, :, first : first + size]
        return row_scale * block.transpose(1, 0, 2).reshape(share, count * size)

    def rotary(heads):
        swapped = jnp.concatenate(
            [heads[..., HEAD_SIZE // 2 :], heads[..., : HEAD_SIZE // 2]], axis=-1
        )
        shape = (share,) + (1,) * (heads.ndim - 2) + (HEAD_SIZE,)
        return (heads * cosine.reshape(shape) + swapped * sine.reshape(shape)).astype(jnp.bfloat16)

    query = rotary(columns(0, query_columns).reshape(share, kv_heads, group, HEAD_SIZE))
    fresh_key = rotary(
        columns(query_columns, key_columns).reshape(share, kv_heads, HEAD_SIZE)
    )
    fresh_value = columns(query_columns + key_columns, key_columns).astype(jnp.bfloat16)
    key_heads = key_rows.reshape(share, slots, kv_heads, HEAD_SIZE)
    value_heads = value_rows.reshape(share, slots, kv_heads, HEAD_SIZE)
    scale = 1.0 / HEAD_SIZE**0.5
    scores = scale * jnp.einsum(
        "nkgd,nlkd->nkgl", query, key_heads, preferred_element_type=jnp.float32
    )
    own = scale * jnp.einsum(
        "nkgd,nkd->nkg", query, fresh_key, preferred_element_type=jnp.float32
    )
    valid = jnp.arange(slots)[None, None, None, :] < lengths[:, None, None, None]
    scores = jnp.where(valid, scores, -1e30)
    top = jnp.maximum(jnp.max(scores, axis=-1), own)
    weights = jnp.where(valid, jnp.exp(scores - top[..., None]), 0.0)
    own_weight = jnp.exp(own - top)
    total = jnp.sum(weights, axis=-1) + own_weight
    mixed = jnp.einsum(
        "nkgl,nlkd->nkgd",
        weights.astype(jnp.bfloat16),
        value_heads,
        preferred_element_type=jnp.float32,
    )
    own_weight = own_weight.astype(jnp.bfloat16).astype(jnp.float32)
    mixed = mixed + own_weight[..., None] * fresh_value.reshape(
        share, kv_heads, 1, HEAD_SIZE
    ).astype(jnp.float32)
    mixed = (mixed / total[..., None]).astype(jnp.bfloat16)
    blocks = mixed.reshape(share, count, query_columns).transpose(1, 0, 2)
    blocks = jnp.take(blocks, order, axis=0)
    return [blocks[offset] for offset in range(count)]


def solution(mesh):
    placed = (
        P(("parts", "gy"), "gx"),
        P("gx"),
        P("gx", "gy"),
        P("gx", "gy"),
        P("gx", "gy"),
        P("gy", "gx"),
        P(("parts", "gx", "gy"), None, None),
        P(("parts", "gx", "gy"), None, None),
        P(("parts", "gx", "gy")),
    )
    return jax.shard_map(
        per_device, mesh=mesh, in_specs=placed, out_specs=P(("parts", "gy"), "gx"), check_vma=False
    )
```

```python
import functools
import math

import jax
import jax.numpy as jnp
from jax import lax
from jax.experimental import pallas as pl
from jax.experimental.pallas import tpu as pltpu
from jax.sharding import PartitionSpec as P

HEAD_SIZE = 128
LANES = 128
EPSILON = 1e-05
ORDERS = {
    "hidden": (2, 3, 1),
    "sum_gx": (2, 1, 3),
    "to_owner": (2, 3, 1),
    "to_head_rows": (2, 3, 1),
    "gather_gx": (2, 1, 3),
    "sum_gy": (2, 1, 3),
}
CUTS = (0, 3, 5, 8)
LOADS = len(CUTS) - 1
VMEM = pl.BlockSpec(memory_space=pltpu.VMEM)


def square_lanes(total):
    high = total.astype(jnp.bfloat16).astype(jnp.float32)
    rest = total - high
    middle = rest.astype(jnp.bfloat16).astype(jnp.float32)
    lane = lax.broadcasted_iota(jnp.int32, (total.shape[0], LANES), 1)
    low = rest - middle
    return jnp.where(lane == 0, high, jnp.where(lane == 1, middle, jnp.where(lane == 2, low, 0.0)))


def padded(left):
    missing = -left.shape[0] % 128
    if not missing:
        return left
    return jnp.concatenate([left, jnp.zeros((missing, left.shape[1]), left.dtype)], axis=0)


def project_kernel(count, width, *refs):
    pieces = [refs[order("hidden", count).index(offset)] for offset in range(count)]
    gain, w_query, key_weight, value_weight = refs[count : count + 4]
    outs, (held,) = refs[count + 4 : 2 * count + 4], refs[2 * count + 4 :]
    flip = lax.axis_index("gx") ^ lax.axis_index("gy") ^ 1
    gains = gain[...].astype(jnp.float32)[None, :]
    rows = pieces[0].shape[0]
    scaled = []
    for offset in range(count):
        states = pieces[offset][...].astype(jnp.float32)
        scaled.append((states * gains).astype(jnp.bfloat16))
        held[flip ^ offset, :, width - LANES :] = square_lanes(
            jnp.sum(states * states, axis=1, keepdims=True)
        ).astype(jnp.bfloat16)
    left = padded(jnp.concatenate(scaled, axis=0))
    start = 0
    for weight in (w_query, key_weight, value_weight):
        columns = weight.shape[1]
        step = min(columns, 512)
        for first in range(0, columns, step):
            product = jnp.dot(
                left, weight[:, first : first + step], preferred_element_type=jnp.float32
            ).astype(jnp.bfloat16)
            for offset in range(count):
                held[flip ^ offset, :, start : start + step] = product[
                    offset * rows : (offset + 1) * rows
                ]
            start += step
    for offset in range(count):
        outs[offset][...] = held[offset]
        if start < width - LANES:
            outs[offset][:, start : width - LANES] = jnp.zeros(
                (rows, width - LANES - start), jnp.bfloat16
            )


def combine_kernel(count, *refs):
    pieces = [refs[order("sum_gx", count).index(offset)] for offset in range(count)]
    outs, (held,) = refs[count : 2 * count], refs[2 * count :]
    total = pieces[0][...].astype(jnp.float32)
    for piece in pieces[1:]:
        total = total + piece[...].astype(jnp.float32)
    share = held.shape[1]
    width = total.shape[1]
    squares = square_lanes(jnp.sum(total[:, width - LANES :], axis=1, keepdims=True))
    for owner in range(count):
        rows = slice(owner * share, (owner + 1) * share)
        held[owner, :, : width - LANES] = total[rows, : width - LANES]
        held[owner, :, width - LANES :] = squares[rows]
    me = lax.axis_index("gy")
    for offset in range(count):
        outs[offset][...] = held[me ^ offset].astype(jnp.bfloat16)


def spread(rows, group):
    repeat = min(group, max(1, 8 // rows.shape[0]))
    tile = jnp.concatenate([rows] * repeat, axis=0) if repeat > 1 else rows
    wide = jnp.broadcast_to(tile[None], (group // repeat, *tile.shape))
    return wide.reshape(group * rows.shape[0], rows.shape[1])


def attend_kernel(offsets, group, features, *refs):
    count = len(offsets)
    pieces = refs[:count]
    keys, values, cosines, sines, filled = refs[count : count + 5]
    outs, rows_of = refs[count + 5 : -1], refs[-1]
    share, slots = keys.shape[0], keys.shape[1]
    rows = share * group
    scale = 1.0 / HEAD_SIZE**0.5
    width = pieces[0].shape[1]
    me = lax.axis_index("gy")
    cosine, sine = cosines[...], sines[...]
    squares = jnp.sum(
        pieces[0][:, width - LANES :].astype(jnp.float32), axis=1, keepdims=True
    )
    row_scale = lax.rsqrt(squares / features + EPSILON)
    row_scales = spread(row_scale, group)
    valid = lax.broadcasted_iota(jnp.int32, (rows, slots), 1) < filled[:, :1]

    def per_head(sequences):
        return jnp.concatenate(
            [
                jnp.broadcast_to(sequences[n : n + 1], (group, HEAD_SIZE))
                for n in range(share)
            ],
            axis=0,
        )

    states, scores = [], []
    for index, offset in enumerate(offsets):
        piece = pieces[index][...].astype(jnp.float32)
        head = me ^ offset
        lanes = pl.ds(pl.multiple_of(head * HEAD_SIZE, HEAD_SIZE), HEAD_SIZE)
        query = jnp.concatenate(
            [piece[:, h * HEAD_SIZE : (h + 1) * HEAD_SIZE] for h in range(group)], axis=0
        )
        query = query * row_scales
        query = query * cosine + pltpu.roll(query, HEAD_SIZE // 2, 1) * sine
        rows_of[index] = query.astype(jnp.bfloat16).astype(jnp.float32)
        first = group * HEAD_SIZE
        fresh_key = piece[:, first : first + HEAD_SIZE] * row_scale
        fresh_key = (
            fresh_key * cosine[:share] + pltpu.roll(fresh_key, HEAD_SIZE // 2, 1) * sine[:share]
        )
        fresh_key = per_head(fresh_key.astype(jnp.bfloat16).astype(jnp.float32))
        first = first + HEAD_SIZE
        fresh_value = piece[:, first : first + HEAD_SIZE] * row_scale
        fresh_value = per_head(fresh_value.astype(jnp.bfloat16).astype(jnp.float32))
        queries = [rows_of[index, pl.ds(n, group, stride=share), :] for n in range(share)]
        own = scale * jnp.sum(
            jnp.concatenate(queries, axis=0) * fresh_key, axis=1, keepdims=True
        )
        states.append((lanes, own, fresh_value))
        score = jnp.concatenate(
            [
                lax.dot_general(
                    queries[n].astype(jnp.bfloat16),
                    keys[n, :, lanes],
                    (((1,), (1,)), ((), ())),
                    preferred_element_type=jnp.float32,
                )
                for n in range(share)
            ],
            axis=0,
        )
        scores.append(jnp.where(valid, score * scale, -1e30))
    tops = [
        jnp.maximum(jnp.max(score, axis=1, keepdims=True), own)
        for score, (_, own, _) in zip(scores, states)
    ]
    weights = [
        jnp.where(valid, jnp.exp(score - top), 0.0) for score, top in zip(scores, tops)
    ]
    for index, (lanes, own, fresh_value) in enumerate(states):
        own_weight = jnp.exp(own - tops[index])
        total = jnp.sum(weights[index], axis=1, keepdims=True) + own_weight
        rounded = weights[index].astype(jnp.bfloat16)
        mixed = jnp.concatenate(
            [
                jnp.dot(
                    rounded[n * group : (n + 1) * group],
                    values[n, :, lanes],
                    preferred_element_type=jnp.float32,
                )
                for n in range(share)
            ],
            axis=0,
        )
        mixed = mixed + own_weight.astype(jnp.bfloat16).astype(jnp.float32) * fresh_value
        mixed = mixed / total
        for n in range(share):
            rows_of[index, pl.ds(n, group, stride=share), :] = mixed[n * group : (n + 1) * group]
        outs[index][...] = jnp.concatenate(
            [rows_of[index, h * share : (h + 1) * share, :] for h in range(group)], axis=1
        ).astype(jnp.bfloat16)


def assemble_kernel(count, *refs):
    pieces = [refs[order("to_head_rows", count).index(offset)] for offset in range(count)]
    out, held = refs[count], refs[count + 1]
    me = lax.axis_index("gy")
    for offset in range(count):
        held[me ^ offset] = pieces[offset][...].astype(jnp.float32)
    out[...] = jnp.concatenate([held[n] for n in range(count)], axis=0).astype(jnp.bfloat16)


def output_kernel(count, *refs):
    pieces = [refs[order("gather_gx", count).index(offset)] for offset in range(count)]
    weights = refs[count : count + LOADS]
    outs, (held,) = refs[count + LOADS : 2 * count + LOADS], refs[2 * count + LOADS :]
    flip = lax.axis_index("gx") ^ lax.axis_index("gy") ^ 1
    for offset in range(count):
        held[flip ^ offset] = pieces[offset][...]
    rows = held.shape[1]
    left = padded(held[...].reshape(count * rows, held.shape[2]))
    columns = weights[0].shape[1]
    step = min(columns, 512)
    for first in range(0, columns, step):
        product, start = 0.0, 0
        for weight in weights:
            depth = weight.shape[0]
            product = product + jnp.dot(
                left[:, start : start + depth],
                weight[:, first : first + step],
                preferred_element_type=jnp.float32,
            )
            start += depth
        product = product.astype(jnp.bfloat16)
        for offset in range(count):
            outs[offset][:, first : first + step] = product[offset * rows : (offset + 1) * rows]


def add_kernel(count, *refs):
    total = refs[0][...].astype(jnp.float32)
    for piece in refs[1:count]:
        total = total + piece[...].astype(jnp.float32)
    refs[count][...] = total.astype(jnp.bfloat16)


def rotary_kernel(share, lengths, cosines, sines, filled):
    rows = cosines.shape[0]
    item = lax.broadcasted_iota(jnp.int32, (rows, HEAD_SIZE), 0) % share
    column = lax.broadcasted_iota(jnp.int32, (rows, HEAD_SIZE), 1)
    half = HEAD_SIZE // 2
    sequence = lax.broadcasted_iota(jnp.int32, (rows, HEAD_SIZE), 0) // (rows // share)
    length = jnp.zeros((rows, HEAD_SIZE), jnp.int32)
    slots = length
    for n in range(share):
        length = jnp.where(item == n, lengths[n], length)
        slots = jnp.where(sequence == n, lengths[n], slots)
    power = (column % half).astype(jnp.float32) * (2.0 / HEAD_SIZE)
    angles = length.astype(jnp.float32) * jnp.exp(-math.log(500000.0) * power)
    sine = jnp.sin(angles)
    cosines[...] = jnp.cos(angles)
    sines[...] = jnp.where(column < half, -sine, sine)
    filled[...] = slots


def loading(kernel, loads, counts, *refs):
    skip, inputs, outputs = counts
    many = len(loads)
    sources, refs = refs[:many], refs[many + skip :]
    if many:
        targets, sems = refs[inputs + outputs : inputs + outputs + many], refs[-1]
        refs = refs[: inputs + outputs] + refs[inputs + outputs + many : -1]
    copies = [
        pltpu.make_async_copy(sources[n].at[pl.ds(first, rows)], targets[n], sems.at[n])
        for n, (first, rows) in enumerate(loads)
    ]
    for copy in copies:
        copy.start()
    if kernel is not None and copies:
        pl.when(lax.axis_index("gy") >= 0)(lambda: kernel(*refs))
    elif kernel is not None:
        kernel(*refs)
    for copy in copies:
        copy.wait()


def call(kernel, outs, scratch, args, name, limit, scalars=0, loads=(), flops=0, after=()):
    arrays = [pltpu.with_memory_space_constraint(load[0], pltpu.HBM) for load in loads]
    parts = [load[1:] for load in loads]
    size = sum(2 * rows * array.shape[1] for array, _, rows in loads)
    results = pl.pallas_call(
        functools.partial(loading, kernel, parts, (len(after), len(args), len(outs))),
        out_shape=[*outs, *(pltpu.VMEM((rows, a.shape[1]), a.dtype) for a, _, rows in loads)],
        in_specs=[pl.BlockSpec(memory_space=pltpu.HBM)] * len(loads)
        + [pl.BlockSpec(memory_space=pl.ANY)] * len(after)
        + [VMEM] * (len(args) - scalars)
        + [pl.BlockSpec(memory_space=pltpu.SMEM)] * scalars,
        out_specs=[VMEM] * (len(outs) + len(loads)),
        scratch_shapes=scratch
        + ([pltpu.SemaphoreType.DMA((len(loads),))] if loads else []),
        cost_estimate=pl.CostEstimate(
            flops=flops, bytes_accessed=2 * size + (1 << 16), transcendentals=0
        ),
        compiler_params=pltpu.CompilerParams(vmem_limit_bytes=limit << 20),
        name=name,
    )(*arrays, *after, *args)
    return results[: len(outs)], results[len(outs) :]


def array(shape, dtype=jnp.bfloat16):
    return jax.ShapeDtypeStruct(shape, dtype)


def order(name, count):
    if count == len(ORDERS[name]) + 1:
        return (0, *ORDERS[name])
    return (0, *range(count - 1, 0, -1))


def exchange(pieces, axis, name):
    count = len(pieces)
    result = list(pieces)
    for offset in order(name, count)[1:]:
        result[offset] = lax.ppermute(
            pieces[offset], axis, [(n, n ^ offset) for n in range(count)]
        )
    return result


def crossing_exchange(pieces, name):
    count = len(pieces)
    result = list(pieces)
    for offset in (*order(name, count)[1:], 0):
        result[offset] = lax.ppermute(
            pieces[offset],
            ("gx", "gy"),
            [(n, (n ^ count) ^ offset) for n in range(lax.axis_size("gx") * count)],
        )
    return result


def per_device(
    hidden_states,
    norm_gain,
    w_query,
    key_weight,
    value_weight,
    w_output,
    stored_key_cache,
    stored_value_cache,
    filled_lengths,
):
    across, down = lax.axis_size("gx"), lax.axis_size("gy")
    assert across == down and across & (across - 1) == 0
    count = down
    share, slots, cache_width = stored_key_cache.shape
    rows, depth = hidden_states.shape
    features = depth * across
    query_columns, key_columns = w_query.shape[1], key_weight.shape[1]
    kv_heads = cache_width // HEAD_SIZE
    group = query_columns * down // HEAD_SIZE // kv_heads

    used = query_columns + 2 * key_columns
    width = -(-used // LANES) * LANES + LANES
    out_rows, out_columns = w_output.shape
    cuts = [out_rows * cut // 8 for cut in CUTS]

    def load(index):
        return w_output, cuts[index], cuts[index + 1] - cuts[index]

    with jax.named_scope("gather_hidden"):
        gathered = exchange([hidden_states] * count, "gy", "hidden")
    with jax.named_scope("fetch_query"):
        _, weights = call(None, [], [], [], "fetch_query", 4, loads=[(w_query, 0, depth)])
    with jax.named_scope("project"):
        partial, output_weights = call(
            functools.partial(project_kernel, count, width),
            [array((rows, width))] * count,
            [pltpu.VMEM((count, rows, width), jnp.bfloat16)],
            [
                *(gathered[k] for k in order("hidden", count)),
                norm_gain,
                *weights,
                key_weight,
                value_weight,
            ],
            "project",
            8,
            loads=[load(0)],
            flops=2 * count * rows * depth * used,
        )
    with jax.named_scope("sum_gx"):
        received = exchange(partial, "gx", "sum_gx")
        table = array((share * group, HEAD_SIZE), jnp.float32)
        (cosine, sine, filled), loaded = call(
            functools.partial(rotary_kernel, share),
            [table, table, array(table.shape, jnp.int32)],
            [],
            [filled_lengths],
            "fetch_output",
            4,
            scalars=1,
            loads=[load(1)],
            after=partial[:1],
        )
        output_weights += loaded
        owned, _ = call(
            functools.partial(combine_kernel, count),
            [array((share, width))] * count,
            [pltpu.VMEM((count, share, width), jnp.float32)],
            [received[k] for k in order("sum_gx", count)],
            "combine",
            4,
            after=output_weights[1:],
        )
    with jax.named_scope("to_owner"):
        owned = crossing_exchange(owned, "to_owner")

    with jax.named_scope("attend"):
        if key_columns == HEAD_SIZE:
            attended = [None] * count
            taken = order("to_owner", count)
            early = len(taken) // 2
            for offsets in (taken[:early], taken[early:]):
                results, _ = call(
                    functools.partial(attend_kernel, offsets, group, features),
                    [array((share, query_columns))] * len(offsets),
                    [pltpu.VMEM((len(offsets), share * group, HEAD_SIZE), jnp.float32)],
                    [
                        *(owned[k] for k in offsets),
                        stored_key_cache,
                        stored_value_cache,
                        cosine,
                        sine,
                        filled,
                    ],
                    "attend",
                    8,
                )
                for offset, result in zip(offsets, results):
                    attended[offset] = result
        else:
            attended = attend_narrow(
                owned, used, features, stored_key_cache, stored_value_cache, cosine[:share],
                sine[:share], filled_lengths, query_columns, key_columns,
            )

    with jax.named_scope("to_head_rows"):
        attended = crossing_exchange(attended, "to_head_rows")
        (block,), _ = call(
            functools.partial(assemble_kernel, count),
            [array((count * share, query_columns))],
            [pltpu.VMEM((count, share, query_columns), jnp.float32)],
            [attended[k] for k in order("to_head_rows", count)],
            "assemble",
            4,
        )
    with jax.named_scope("gather_gx"):
        blocks = exchange([block] * count, "gx", "gather_gx")
        output_weights += call(
            None, [], [], [], "fetch_output", 4, loads=[load(2)], after=[block]
        )[1]
    with jax.named_scope("output"):
        products, _ = call(
            functools.partial(output_kernel, count),
            [array((count * share, out_columns))] * count,
            [pltpu.VMEM((count, count * share, query_columns), jnp.bfloat16)],
            [*(blocks[k] for k in order("gather_gx", count)), *output_weights],
            "output",
            8,
            flops=2 * count * count * share * out_rows * out_columns,
        )
    with jax.named_scope("sum_gy"):
        products = exchange(products, "gy", "sum_gy")
        (result,), _ = call(
            functools.partial(add_kernel, count),
            [array((rows, out_columns))],
            [],
            [products[k] for k in order("sum_gy", count)],
            "add",
            8,
        )
        return result


def attend_narrow(
    owned, used, features, key_rows, value_rows, cosine, sine, lengths, query_columns, key_columns
):
    count = len(owned)
    share, slots, cache_width = key_rows.shape
    kv_heads = cache_width // HEAD_SIZE
    group = query_columns * count // HEAD_SIZE // kv_heads
    me = lax.axis_index("gy")
    order = me ^ jnp.arange(count)
    stacked = jnp.stack(owned).astype(jnp.float32)
    squares = jnp.sum(stacked[0, :, -LANES:], axis=1)
    row_scale = lax.rsqrt(squares / features + EPSILON)[:, None]
    stacked = jnp.take(stacked, order, axis=0)

    def columns(first, size):
        block = stacked[:, :, first : first + size]
        return row_scale * block.transpose(1, 0, 2).reshape(share, count * size)

    def rotary(heads):
        swapped = jnp.concatenate(
            [heads[..., HEAD_SIZE // 2 :], heads[..., : HEAD_SIZE // 2]], axis=-1
        )
        shape = (share,) + (1,) * (heads.ndim - 2) + (HEAD_SIZE,)
        return (heads * cosine.reshape(shape) + swapped * sine.reshape(shape)).astype(jnp.bfloat16)

    query = rotary(columns(0, query_columns).reshape(share, kv_heads, group, HEAD_SIZE))
    fresh_key = rotary(
        columns(query_columns, key_columns).reshape(share, kv_heads, HEAD_SIZE)
    )
    fresh_value = columns(query_columns + key_columns, key_columns).astype(jnp.bfloat16)
    key_heads = key_rows.reshape(share, slots, kv_heads, HEAD_SIZE)
    value_heads = value_rows.reshape(share, slots, kv_heads, HEAD_SIZE)
    scale = 1.0 / HEAD_SIZE**0.5
    scores = scale * jnp.einsum(
        "nkgd,nlkd->nkgl", query, key_heads, preferred_element_type=jnp.float32
    )
    own = scale * jnp.einsum(
        "nkgd,nkd->nkg", query, fresh_key, preferred_element_type=jnp.float32
    )
    valid = jnp.arange(slots)[None, None, None, :] < lengths[:, None, None, None]
    scores = jnp.where(valid, scores, -1e30)
    top = jnp.maximum(jnp.max(scores, axis=-1), own)
    weights = jnp.where(valid, jnp.exp(scores - top[..., None]), 0.0)
    own_weight = jnp.exp(own - top)
    total = jnp.sum(weights, axis=-1) + own_weight
    mixed = jnp.einsum(
        "nkgl,nlkd->nkgd",
        weights.astype(jnp.bfloat16),
        value_heads,
        preferred_element_type=jnp.float32,
    )
    own_weight = own_weight.astype(jnp.bfloat16).astype(jnp.float32)
    mixed = mixed + own_weight[..., None] * fresh_value.reshape(
        share, kv_heads, 1, HEAD_SIZE
    ).astype(jnp.float32)
    mixed = (mixed / total[..., None]).astype(jnp.bfloat16)
    blocks = mixed.reshape(share, count, query_columns).transpose(1, 0, 2)
    blocks = jnp.take(blocks, order, axis=0)
    return [blocks[offset] for offset in range(count)]


def solution(mesh):
    placed = (
        P(("parts", "gy"), "gx"),
        P("gx"),
        P("gx", "gy"),
        P("gx", "gy"),
        P("gx", "gy"),
        P("gy", "gx"),
        P(("parts", "gx", "gy"), None, None),
        P(("parts", "gx", "gy"), None, None),
        P(("parts", "gx", "gy")),
    )
    return jax.shard_map(
        per_device, mesh=mesh, in_specs=placed, out_specs=P(("parts", "gy"), "gx"), check_vma=False
    )
```

```python
import functools
import math

import jax
import jax.numpy as jnp
from jax import lax
from jax.experimental import pallas as pl
from jax.experimental.pallas import tpu as pltpu
from jax.sharding import PartitionSpec as P

HEAD_SIZE = 128
LANES = 128
EPSILON = 1e-05
ORDERS = {
    "hidden": (2, 3, 1),
    "sum_gx": (2, 1, 3),
    "to_owner": (2, 3, 1),
    "to_head_rows": (2, 3, 1),
    "gather_gx": (2, 1, 3),
    "sum_gy": (2, 1, 3),
}
CUTS = (0, 3, 5, 8)
LOADS = len(CUTS) - 1
VMEM = pl.BlockSpec(memory_space=pltpu.VMEM)


def square_lanes(total):
    high = total.astype(jnp.bfloat16).astype(jnp.float32)
    rest = total - high
    middle = rest.astype(jnp.bfloat16).astype(jnp.float32)
    lane = lax.broadcasted_iota(jnp.int32, (total.shape[0], LANES), 1)
    low = rest - middle
    return jnp.where(lane == 0, high, jnp.where(lane == 1, middle, jnp.where(lane == 2, low, 0.0)))


def padded(left):
    missing = -left.shape[0] % 128
    if not missing:
        return left
    return jnp.concatenate([left, jnp.zeros((missing, left.shape[1]), left.dtype)], axis=0)


def project_kernel(count, width, *refs):
    pieces = [refs[order("hidden", count).index(offset)] for offset in range(count)]
    gain, w_query, key_weight, value_weight = refs[count : count + 4]
    outs, (held,) = refs[count + 4 : 2 * count + 4], refs[2 * count + 4 :]
    flip = lax.axis_index("gx") ^ lax.axis_index("gy") ^ 1
    gains = gain[...].astype(jnp.float32)[None, :]
    rows = pieces[0].shape[0]
    scaled = []
    for offset in range(count):
        states = pieces[offset][...].astype(jnp.float32)
        scaled.append((states * gains).astype(jnp.bfloat16))
        held[flip ^ offset, :, width - LANES :] = square_lanes(
            jnp.sum(states * states, axis=1, keepdims=True)
        ).astype(jnp.bfloat16)
    left = padded(jnp.concatenate(scaled, axis=0))
    start = 0
    for weight in (w_query, key_weight, value_weight):
        columns = weight.shape[1]
        step = min(columns, 512)
        for first in range(0, columns, step):
            product = jnp.dot(
                left, weight[:, first : first + step], preferred_element_type=jnp.float32
            ).astype(jnp.bfloat16)
            for offset in range(count):
                held[flip ^ offset, :, start : start + step] = product[
                    offset * rows : (offset + 1) * rows
                ]
            start += step
    for offset in range(count):
        outs[offset][...] = held[offset]
        if start < width - LANES:
            outs[offset][:, start : width - LANES] = jnp.zeros(
                (rows, width - LANES - start), jnp.bfloat16
            )


def combine_kernel(count, *refs):
    pieces = [refs[order("sum_gx", count).index(offset)] for offset in range(count)]
    outs, (held,) = refs[count : 2 * count], refs[2 * count :]
    total = pieces[0][...].astype(jnp.float32)
    for piece in pieces[1:]:
        total = total + piece[...].astype(jnp.float32)
    share = held.shape[1]
    width = total.shape[1]
    squares = square_lanes(jnp.sum(total[:, width - LANES :], axis=1, keepdims=True))
    for owner in range(count):
        rows = slice(owner * share, (owner + 1) * share)
        held[owner, :, : width - LANES] = total[rows, : width - LANES]
        held[owner, :, width - LANES :] = squares[rows]
    me = lax.axis_index("gy")
    for offset in range(count):
        outs[offset][...] = held[me ^ offset].astype(jnp.bfloat16)


def attend_kernel(offsets, group, features, *refs):
    count = len(offsets)
    pieces = refs[:count]
    keys, values, cosines, sines, filled = refs[count : count + 5]
    outs, rows_of = refs[count + 5 : -1], refs[-1]
    share, slots = keys.shape[0], keys.shape[1]
    rows = share * group
    scale = 1.0 / HEAD_SIZE**0.5
    width = pieces[0].shape[1]
    me = lax.axis_index("gy")
    cosine, sine = cosines[...], sines[...]
    squares = jnp.sum(
        pieces[0][:, width - LANES :].astype(jnp.float32), axis=1, keepdims=True
    )
    row_scale = lax.rsqrt(squares / features + EPSILON)
    valid = lax.broadcasted_iota(jnp.int32, (rows, slots), 1) < filled[:, :1]

    def per_head(sequences):
        return jnp.concatenate(
            [
                jnp.broadcast_to(sequences[n : n + 1], (group, HEAD_SIZE))
                for n in range(share)
            ],
            axis=0,
        )

    states, scores = [], []
    for index, offset in enumerate(offsets):
        piece = pieces[index][...].astype(jnp.float32) * row_scale
        head = me ^ offset
        lanes = pl.ds(pl.multiple_of(head * HEAD_SIZE, HEAD_SIZE), HEAD_SIZE)
        query = jnp.concatenate(
            [piece[:, h * HEAD_SIZE : (h + 1) * HEAD_SIZE] for h in range(group)], axis=0
        )
        query = query * cosine + pltpu.roll(query, HEAD_SIZE // 2, 1) * sine
        rows_of[index] = query.astype(jnp.bfloat16).astype(jnp.float32)
        first = group * HEAD_SIZE
        fresh_key = piece[:, first : first + HEAD_SIZE]
        fresh_key = (
            fresh_key * cosine[:share] + pltpu.roll(fresh_key, HEAD_SIZE // 2, 1) * sine[:share]
        )
        fresh_key = per_head(fresh_key.astype(jnp.bfloat16).astype(jnp.float32))
        first = first + HEAD_SIZE
        fresh_value = piece[:, first : first + HEAD_SIZE]
        fresh_value = per_head(fresh_value.astype(jnp.bfloat16).astype(jnp.float32))
        queries = [rows_of[index, pl.ds(n, group, stride=share), :] for n in range(share)]
        own = scale * jnp.sum(
            jnp.concatenate(queries, axis=0) * fresh_key, axis=1, keepdims=True
        )
        states.append((lanes, own, fresh_value))
        score = jnp.concatenate(
            [
                lax.dot_general(
                    queries[n].astype(jnp.bfloat16),
                    keys[n, :, lanes],
                    (((1,), (1,)), ((), ())),
                    preferred_element_type=jnp.float32,
                )
                for n in range(share)
            ],
            axis=0,
        )
        scores.append(jnp.where(valid, score * scale, -1e30))
    tops = [
        jnp.maximum(jnp.max(score, axis=1, keepdims=True), own)
        for score, (_, own, _) in zip(scores, states)
    ]
    weights = [
        jnp.where(valid, jnp.exp(score - top), 0.0) for score, top in zip(scores, tops)
    ]
    for index, (lanes, own, fresh_value) in enumerate(states):
        own_weight = jnp.exp(own - tops[index])
        total = jnp.sum(weights[index], axis=1, keepdims=True) + own_weight
        rounded = weights[index].astype(jnp.bfloat16)
        mixed = jnp.concatenate(
            [
                jnp.dot(
                    rounded[n * group : (n + 1) * group],
                    values[n, :, lanes],
                    preferred_element_type=jnp.float32,
                )
                for n in range(share)
            ],
            axis=0,
        )
        mixed = mixed + own_weight.astype(jnp.bfloat16).astype(jnp.float32) * fresh_value
        mixed = mixed / total
        for n in range(share):
            rows_of[index, pl.ds(n, group, stride=share), :] = mixed[n * group : (n + 1) * group]
        outs[index][...] = jnp.concatenate(
            [rows_of[index, h * share : (h + 1) * share, :] for h in range(group)], axis=1
        ).astype(jnp.bfloat16)


def assemble_kernel(count, *refs):
    pieces = [refs[order("to_head_rows", count).index(offset)] for offset in range(count)]
    out, held = refs[count], refs[count + 1]
    me = lax.axis_index("gy")
    for offset in range(count):
        held[me ^ offset] = pieces[offset][...].astype(jnp.float32)
    out[...] = jnp.concatenate([held[n] for n in range(count)], axis=0).astype(jnp.bfloat16)


def output_kernel(count, *refs):
    pieces = [refs[order("gather_gx", count).index(offset)] for offset in range(count)]
    weights = refs[count : count + LOADS]
    outs, (held,) = refs[count + LOADS : 2 * count + LOADS], refs[2 * count + LOADS :]
    flip = lax.axis_index("gx") ^ lax.axis_index("gy") ^ 1
    for offset in range(count):
        held[flip ^ offset] = pieces[offset][...]
    rows = held.shape[1]
    left = padded(held[...].reshape(count * rows, held.shape[2]))
    columns = weights[0].shape[1]
    step = min(columns, 512)
    for first in range(0, columns, step):
        product, start = 0.0, 0
        for weight in weights:
            depth = weight.shape[0]
            product = product + jnp.dot(
                left[:, start : start + depth],
                weight[:, first : first + step],
                preferred_element_type=jnp.float32,
            )
            start += depth
        product = product.astype(jnp.bfloat16)
        for offset in range(count):
            outs[offset][:, first : first + step] = product[offset * rows : (offset + 1) * rows]


def add_kernel(count, *refs):
    total = refs[0][...].astype(jnp.float32)
    for piece in refs[1:count]:
        total = total + piece[...].astype(jnp.float32)
    refs[count][...] = total.astype(jnp.bfloat16)


def rotary_kernel(share, lengths, cosines, sines, filled):
    rows = cosines.shape[0]
    item = lax.broadcasted_iota(jnp.int32, (rows, HEAD_SIZE), 0) % share
    column = lax.broadcasted_iota(jnp.int32, (rows, HEAD_SIZE), 1)
    half = HEAD_SIZE // 2
    sequence = lax.broadcasted_iota(jnp.int32, (rows, HEAD_SIZE), 0) // (rows // share)
    length = jnp.zeros((rows, HEAD_SIZE), jnp.int32)
    slots = length
    for n in range(share):
        length = jnp.where(item == n, lengths[n], length)
        slots = jnp.where(sequence == n, lengths[n], slots)
    power = (column % half).astype(jnp.float32) * (2.0 / HEAD_SIZE)
    angles = length.astype(jnp.float32) * jnp.exp(-math.log(500000.0) * power)
    sine = jnp.sin(angles)
    cosines[...] = jnp.cos(angles)
    sines[...] = jnp.where(column < half, -sine, sine)
    filled[...] = slots


def loading(kernel, loads, counts, *refs):
    skip, inputs, outputs = counts
    many = len(loads)
    sources, refs = refs[:many], refs[many + skip :]
    if many:
        targets, sems = refs[inputs + outputs : inputs + outputs + many], refs[-1]
        refs = refs[: inputs + outputs] + refs[inputs + outputs + many : -1]
    copies = [
        pltpu.make_async_copy(sources[n].at[pl.ds(first, rows)], targets[n], sems.at[n])
        for n, (first, rows) in enumerate(loads)
    ]
    for copy in copies:
        copy.start()
    if kernel is not None and copies:
        pl.when(lax.axis_index("gy") >= 0)(lambda: kernel(*refs))
    elif kernel is not None:
        kernel(*refs)
    for copy in copies:
        copy.wait()


def call(kernel, outs, scratch, args, name, limit, scalars=0, loads=(), flops=0, after=()):
    arrays = [pltpu.with_memory_space_constraint(load[0], pltpu.HBM) for load in loads]
    parts = [load[1:] for load in loads]
    size = sum(2 * rows * array.shape[1] for array, _, rows in loads)
    results = pl.pallas_call(
        functools.partial(loading, kernel, parts, (len(after), len(args), len(outs))),
        out_shape=[*outs, *(pltpu.VMEM((rows, a.shape[1]), a.dtype) for a, _, rows in loads)],
        in_specs=[pl.BlockSpec(memory_space=pltpu.HBM)] * len(loads)
        + [pl.BlockSpec(memory_space=pl.ANY)] * len(after)
        + [VMEM] * (len(args) - scalars)
        + [pl.BlockSpec(memory_space=pltpu.SMEM)] * scalars,
        out_specs=[VMEM] * (len(outs) + len(loads)),
        scratch_shapes=scratch
        + ([pltpu.SemaphoreType.DMA((len(loads),))] if loads else []),
        cost_estimate=pl.CostEstimate(
            flops=flops, bytes_accessed=2 * size + (1 << 16), transcendentals=0
        ),
        compiler_params=pltpu.CompilerParams(vmem_limit_bytes=limit << 20),
        name=name,
    )(*arrays, *after, *args)
    return results[: len(outs)], results[len(outs) :]


def array(shape, dtype=jnp.bfloat16):
    return jax.ShapeDtypeStruct(shape, dtype)


def order(name, count):
    if count == len(ORDERS[name]) + 1:
        return (0, *ORDERS[name])
    return (0, *range(count - 1, 0, -1))


def exchange(pieces, axis, name):
    count = len(pieces)
    result = list(pieces)
    for offset in order(name, count)[1:]:
        result[offset] = lax.ppermute(
            pieces[offset], axis, [(n, n ^ offset) for n in range(count)]
        )
    return result


def crossing_exchange(pieces, name):
    count = len(pieces)
    result = list(pieces)
    for offset in (*order(name, count)[1:], 0):
        result[offset] = lax.ppermute(
            pieces[offset],
            ("gx", "gy"),
            [(n, (n ^ count) ^ offset) for n in range(lax.axis_size("gx") * count)],
        )
    return result


def per_device(
    hidden_states,
    norm_gain,
    w_query,
    key_weight,
    value_weight,
    w_output,
    stored_key_cache,
    stored_value_cache,
    filled_lengths,
):
    across, down = lax.axis_size("gx"), lax.axis_size("gy")
    assert across == down and across & (across - 1) == 0
    count = down
    share, slots, cache_width = stored_key_cache.shape
    rows, depth = hidden_states.shape
    features = depth * across
    query_columns, key_columns = w_query.shape[1], key_weight.shape[1]
    kv_heads = cache_width // HEAD_SIZE
    group = query_columns * down // HEAD_SIZE // kv_heads

    used = query_columns + 2 * key_columns
    width = -(-used // LANES) * LANES + LANES
    out_rows, out_columns = w_output.shape
    cuts = [out_rows * cut // 8 for cut in CUTS]

    def load(index):
        return w_output, cuts[index], cuts[index + 1] - cuts[index]

    with jax.named_scope("gather_hidden"):
        gathered = exchange([hidden_states] * count, "gy", "hidden")
    with jax.named_scope("fetch_query"):
        _, weights = call(None, [], [], [], "fetch_query", 4, loads=[(w_query, 0, depth)])
    with jax.named_scope("project"):
        partial, output_weights = call(
            functools.partial(project_kernel, count, width),
            [array((rows, width))] * count,
            [pltpu.VMEM((count, rows, width), jnp.bfloat16)],
            [
                *(gathered[k] for k in order("hidden", count)),
                norm_gain,
                *weights,
                key_weight,
                value_weight,
            ],
            "project",
            8,
            loads=[load(0)],
            flops=2 * count * rows * depth * used,
        )
    with jax.named_scope("sum_gx"):
        received = exchange(partial, "gx", "sum_gx")
        table = array((share * group, HEAD_SIZE), jnp.float32)
        (cosine, sine, filled), loaded = call(
            functools.partial(rotary_kernel, share),
            [table, table, array(table.shape, jnp.int32)],
            [],
            [filled_lengths],
            "fetch_output",
            4,
            scalars=1,
            loads=[load(1)],
            after=partial[:1],
        )
        output_weights += loaded
        owned, _ = call(
            functools.partial(combine_kernel, count),
            [array((share, width))] * count,
            [pltpu.VMEM((count, share, width), jnp.float32)],
            [received[k] for k in order("sum_gx", count)],
            "combine",
            4,
            after=output_weights[1:],
        )
    with jax.named_scope("to_owner"):
        owned = crossing_exchange(owned, "to_owner")

    with jax.named_scope("attend"):
        if key_columns == HEAD_SIZE:
            attended = [None] * count
            taken = order("to_owner", count)
            early = len(taken) // 2
            for offsets in (taken[:early], taken[early:]):
                results, _ = call(
                    functools.partial(attend_kernel, offsets, group, features),
                    [array((share, query_columns))] * len(offsets),
                    [pltpu.VMEM((len(offsets), share * group, HEAD_SIZE), jnp.float32)],
                    [
                        *(owned[k] for k in offsets),
                        stored_key_cache,
                        stored_value_cache,
                        cosine,
                        sine,
                        filled,
                    ],
                    "attend",
                    8,
                )
                for offset, result in zip(offsets, results):
                    attended[offset] = result
        else:
            attended = attend_narrow(
                owned, used, features, stored_key_cache, stored_value_cache, cosine[:share],
                sine[:share], filled_lengths, query_columns, key_columns,
            )

    with jax.named_scope("to_head_rows"):
        attended = crossing_exchange(attended, "to_head_rows")
        (block,), _ = call(
            functools.partial(assemble_kernel, count),
            [array((count * share, query_columns))],
            [pltpu.VMEM((count, share, query_columns), jnp.float32)],
            [attended[k] for k in order("to_head_rows", count)],
            "assemble",
            4,
        )
    with jax.named_scope("gather_gx"):
        blocks = exchange([block] * count, "gx", "gather_gx")
        output_weights += call(
            None, [], [], [], "fetch_output", 4, loads=[load(2)], after=[block]
        )[1]
    with jax.named_scope("output"):
        products, _ = call(
            functools.partial(output_kernel, count),
            [array((count * share, out_columns))] * count,
            [pltpu.VMEM((count, count * share, query_columns), jnp.bfloat16)],
            [*(blocks[k] for k in order("gather_gx", count)), *output_weights],
            "output",
            8,
            flops=2 * count * count * share * out_rows * out_columns,
        )
    with jax.named_scope("sum_gy"):
        products = exchange(products, "gy", "sum_gy")
        (result,), _ = call(
            functools.partial(add_kernel, count),
            [array((rows, out_columns))],
            [],
            [products[k] for k in order("sum_gy", count)],
            "add",
            8,
        )
        return result


def attend_narrow(
    owned, used, features, key_rows, value_rows, cosine, sine, lengths, query_columns, key_columns
):
    count = len(owned)
    share, slots, cache_width = key_rows.shape
    kv_heads = cache_width // HEAD_SIZE
    group = query_columns * count // HEAD_SIZE // kv_heads
    me = lax.axis_index("gy")
    order = me ^ jnp.arange(count)
    stacked = jnp.stack(owned).astype(jnp.float32)
    squares = jnp.sum(stacked[0, :, -LANES:], axis=1)
    row_scale = lax.rsqrt(squares / features + EPSILON)[:, None]
    stacked = jnp.take(stacked, order, axis=0)

    def columns(first, size):
        block = stacked[:, :, first : first + size]
        return row_scale * block.transpose(1, 0, 2).reshape(share, count * size)

    def rotary(heads):
        swapped = jnp.concatenate(
            [heads[..., HEAD_SIZE // 2 :], heads[..., : HEAD_SIZE // 2]], axis=-1
        )
        shape = (share,) + (1,) * (heads.ndim - 2) + (HEAD_SIZE,)
        return (heads * cosine.reshape(shape) + swapped * sine.reshape(shape)).astype(jnp.bfloat16)

    query = rotary(columns(0, query_columns).reshape(share, kv_heads, group, HEAD_SIZE))
    fresh_key = rotary(
        columns(query_columns, key_columns).reshape(share, kv_heads, HEAD_SIZE)
    )
    fresh_value = columns(query_columns + key_columns, key_columns).astype(jnp.bfloat16)
    key_heads = key_rows.reshape(share, slots, kv_heads, HEAD_SIZE)
    value_heads = value_rows.reshape(share, slots, kv_heads, HEAD_SIZE)
    scale = 1.0 / HEAD_SIZE**0.5
    scores = scale * jnp.einsum(
        "nkgd,nlkd->nkgl", query, key_heads, preferred_element_type=jnp.float32
    )
    own = scale * jnp.einsum(
        "nkgd,nkd->nkg", query, fresh_key, preferred_element_type=jnp.float32
    )
    valid = jnp.arange(slots)[None, None, None, :] < lengths[:, None, None, None]
    scores = jnp.where(valid, scores, -1e30)
    top = jnp.maximum(jnp.max(scores, axis=-1), own)
    weights = jnp.where(valid, jnp.exp(scores - top[..., None]), 0.0)
    own_weight = jnp.exp(own - top)
    total = jnp.sum(weights, axis=-1) + own_weight
    mixed = jnp.einsum(
        "nkgl,nlkd->nkgd",
        weights.astype(jnp.bfloat16),
        value_heads,
        preferred_element_type=jnp.float32,
    )
    own_weight = own_weight.astype(jnp.bfloat16).astype(jnp.float32)
    mixed = mixed + own_weight[..., None] * fresh_value.reshape(
        share, kv_heads, 1, HEAD_SIZE
    ).astype(jnp.float32)
    mixed = (mixed / total[..., None]).astype(jnp.bfloat16)
    blocks = mixed.reshape(share, count, query_columns).transpose(1, 0, 2)
    blocks = jnp.take(blocks, order, axis=0)
    return [blocks[offset] for offset in range(count)]


def solution(mesh):
    placed = (
        P(("parts", "gy"), "gx"),
        P("gx"),
        P("gx", "gy"),
        P("gx", "gy"),
        P("gx", "gy"),
        P("gy", "gx"),
        P(("parts", "gx", "gy"), None, None),
        P(("parts", "gx", "gy"), None, None),
        P(("parts", "gx", "gy")),
    )
    return jax.shard_map(
        per_device, mesh=mesh, in_specs=placed, out_specs=P(("parts", "gy"), "gx"), check_vma=False
    )
```
